128 devices in a mesh: wide: 32 (over x, y_hi, z), narrow: 4 (over y_lo, core).
Axes of the slice: x: 4, y: 4 (y_hi: 2, y_lo: 2; y = y_hi * 2 + y_lo), z: 4, core: 2. Of those that a mesh axis runs over, the one named last changes fastest.
Arguments:
- field: float32 [4, 512, 256, 512], P(None, 'narrow', 'wide'), may hold values from -200 to 200, as said below
- start: float32 [512, 128], replicated, may hold values from -6 to 6
Outputs:
- basis: float32 [512, 128], replicated
- core: float32 [128, 4, 256, 512], P('narrow', None, 'wide')
The draws below stay inside these ranges and needn't reach their ends.
Inputs may be any that keep to these rules, and one draw needn't show every extreme that they name: `field`: every entry is finite; different x rows and species have different scales.
All inputs are finite; a program needn't handle non-finite values.
Results may differ from the reference program's by a relative error of at most 0.0003.
Values sent between devices are 32-bit elements; how exact they have to be, the bound alone decides.
No kernel may reach another device: no remote copies, remote signals or barrier semaphores. Data moves between devices by JAX's collectives and lax.ppermute only.
A program may use at most 64 MiB of HBM per device.

```python
import jax
import jax.numpy as jnp
from jax import lax

S = 4
NX = 512
RANK = 128
NZ = 512
ITERS = 3
NY = 256


def draw_field(key, part):
    keys = jax.random.split(jax.random.fold_in(key, 11), 2)
    row_scale = jnp.exp(jax.random.uniform(keys[0], (S, NX, 1, 1), jnp.float32) * jnp.log(10.0))
    ramp = jnp.arange(NY, dtype=jnp.float32) / max(NY - 1, 1)
    y_scale = jnp.exp(ramp * jnp.log(3.0)).reshape(1, 1, NY, 1)
    noise = jax.random.normal(keys[1], (S, NX, NY, NZ), jnp.float32)
    noise = jnp.clip(noise, -6.0, 6.0)
    return noise * row_scale * y_scale


def normal_values(key, dims, deviation, bound, kind=jnp.bfloat16):
    return jnp.clip(deviation * jax.random.normal(key, dims, jnp.float32), -bound, bound).astype(kind)


def setup_inputs(seed: int = 0) -> dict:
    key_list = jax.random.split(jax.random.key(seed), 3)
    field = draw_field(jax.random.fold_in(key_list[2], 71), 0)
    start = normal_values(key_list[1], (NX, RANK), 1.0, 6.0, jnp.float32)
    return dict(field=field, start=start)


def reference(field, start):
    total = jnp.zeros((NX, NX), jnp.float32)
    for spec in range(S):
        flat = field[spec].reshape(NX, NY * NZ)
        total = total + jnp.dot(flat.astype(jnp.float32), flat.T.astype(jnp.float32), preferred_element_type=jnp.float32, precision=lax.Precision.HIGHEST)
    gram = total / (S * NY * NZ)
    basis = start
    for step in range(ITERS):
        product = jnp.dot(gram.astype(jnp.float32), basis.astype(jnp.float32), preferred_element_type=jnp.float32, precision=lax.Precision.HIGHEST)
        cross = jnp.dot(product.T.astype(jnp.float32), product.astype(jnp.float32), preferred_element_type=jnp.float32, precision=lax.Precision.HIGHEST)
        lower = jnp.linalg.cholesky(cross)
        basis = jax.scipy.linalg.solve_triangular(lower, product.T, lower=True).T
    cores = []
    for spec in range(S):
        flat = field[spec].reshape(NX, NY * NZ)
        cores.append(jnp.dot(basis.T.astype(jnp.float32), flat.astype(jnp.float32), preferred_element_type=jnp.float32, precision=lax.Precision.HIGHEST).reshape(RANK, NY, NZ))
    core = jnp.stack(cores, axis=1)
    return (basis, core)
```

```python
import jax
import jax.numpy as jnp
from jax import lax
from jax.experimental import pallas as pl
from jax.experimental.pallas import tpu as pltpu
from jax.sharding import PartitionSpec as P

ITERS = 3
HIGHEST = lax.Precision.HIGHEST
F32 = jnp.float32
BF16 = jnp.bfloat16
VMEM_LIMIT = 56 * 1024 * 1024


def contract_lanes(a, b):
    return lax.dot_general(a, b, (((1,), (1,)), ((), ())), preferred_element_type=F32)


def split(value):
    hi = value.astype(BF16)
    return hi, (value - hi.astype(F32)).astype(BF16)


def pair(first, second):
    return split(jnp.concatenate([first, second], axis=0))


def store_in_order(out, total, swapped, turned):
    half = total.shape[0] // 2
    for core in (0, 1):
        for turn in (0, 1):

            @pl.when((swapped == core) & (turned == turn))
            def _(core=core, turn=turn):
                value = total.T if turn else total
                if core:
                    out[:half, :half] = value[half:, half:]
                    out[:half, half:] = value[half:, :half]
                    out[half:, :half] = value[:half, half:]
                    out[half:, half:] = value[:half, :half]
                else:
                    out[...] = value


def same_kernel(where, own0, own2, near0, near2, out, main, cross):
    main[...] = jnp.zeros_like(main)
    cross[...] = jnp.zeros_like(cross)
    for own, near in ((own0, near0), (own2, near2)):
        for y in range(own.shape[0]):
            hi, lo = pair(own[y], near[y])
            main[...] += contract_lanes(hi, hi)
            cross[...] += contract_lanes(hi, lo)
    store_in_order(out, main[...] + cross[...] + cross[...].T, where[0] % 2, 0)


def other_kernel(where, own, near, far2, far3, out, main, cross):
    main[...] = jnp.zeros_like(main)
    cross[...] = jnp.zeros_like(cross)
    for y in range(own.shape[0]):
        hi, lo = pair(own[y], near[y])
        far_hi, far_lo = pair(far2[y], far3[y])
        main[...] += contract_lanes(hi, far_hi)
        cross[...] += contract_lanes(hi, far_lo)
        cross[...] += contract_lanes(lo, far_hi)
    store_in_order(out, main[...] + cross[...], where[0] % 2, where[0] // 2)


def panel(rows, inverse, block):
    shape = rows.shape
    sub = lax.broadcasted_iota(jnp.int32, shape, 0)
    cols = [jnp.broadcast_to(rows[:, 8 * block + m : 8 * block + m + 1], shape) for m in range(8)]
    pivots = jnp.ones(shape, F32)
    for j in range(8):
        pivot = jnp.broadcast_to(cols[j][j : j + 1], shape)
        pivots = jnp.where(sub == j, pivot, pivots)
        if j < 7:
            factor = jnp.where(sub > j, cols[j] / pivot, 0.0)
            for m in range(j + 1, 8):
                cols[m] = cols[m] - factor * jnp.broadcast_to(cols[m][j : j + 1], shape)
            rows = rows - factor * jnp.broadcast_to(rows[j : j + 1], shape)
            inverse = inverse - factor * jnp.broadcast_to(inverse[j : j + 1], shape)
    scale = lax.rsqrt(pivots)
    return rows * scale, inverse * scale


def inverse_factor(cross, work):
    rank = cross.shape[0]
    row = lax.broadcasted_iota(jnp.int32, cross.shape, 0)
    col = lax.broadcasted_iota(jnp.int32, cross.shape, 1)
    work[:, :rank] = cross
    work[:, rank:] = jnp.where(row == col, 1.0, 0.0)
    for block in range(rank // 8):
        at = pl.ds(8 * block, 8)
        upper, inverse = panel(work[at, :rank], work[at, rank:], block)
        work[at, rank:] = inverse
        after = 8 * block + 8
        if after < rank:
            both = jnp.concatenate([upper, inverse], axis=1)
            update = lax.dot_general(
                upper, both, (((0,), (0,)), ((), ())), precision=HIGHEST, preferred_element_type=F32
            )
            work[after:, :] -= update[after:]
    return work[:, rank:]


def iterate_kernel(count, g00, g11, g01, start, basis, turned, gram, work):
    half = g00.shape[0]
    scale = 1.0 / count
    gram[:half, :half] = g00[...] * scale
    gram[half:, half:] = g11[...] * scale
    gram[:half, half:] = g01[...] * scale
    gram[half:, :half] = g01[...].T * scale
    now = start[...]
    for _ in range(ITERS):
        product = jnp.dot(gram[...], now, precision=HIGHEST, preferred_element_type=F32)
        cross = lax.dot_general(
            product, product, (((0,), (0,)), ((), ())), precision=HIGHEST, preferred_element_type=F32
        )
        inverse = inverse_factor(cross, work)
        now = lax.dot_general(
            product, inverse, (((1,), (1,)), ((), ())), precision=HIGHEST, preferred_element_type=F32
        )
    basis[...] = now
    turned[...] = now.T


def project_kernel(ranks, where, turned, own, near, far2, far3, out_a, out_b):
    here = where[0]
    cells_y, rows, _ = own.shape
    share = turned.shape[0] // 4
    lines = []
    for rank in ranks:
        line = pl.ds(pl.multiple_of((here ^ rank) * share, share), share)
        cols = [turned[line, pl.ds(pl.multiple_of((here ^ k) * rows, rows), rows)] for k in range(4)]
        lines.append(jnp.concatenate(cols, axis=1))
    b_hi, b_lo = split(jnp.concatenate(lines, axis=0))
    b_both = jnp.concatenate([b_hi, b_lo], axis=0)
    for y in range(cells_y):
        f_hi, f_lo = split(jnp.concatenate([own[y], near[y], far2[y], far3[y]], axis=0))
        with_hi = jnp.dot(b_both, f_hi, preferred_element_type=F32)
        with_lo = jnp.dot(b_hi, f_lo, preferred_element_type=F32)
        total = with_hi[: 2 * share] + with_hi[2 * share :] + with_lo
        out_a[y] = total[:share]
        out_b[y] = total[share:]


def call(kernel, outs, scratch, scalars, args, flops, moved):
    smem = pl.BlockSpec(memory_space=pltpu.SMEM)
    vmem = pl.BlockSpec(memory_space=pltpu.VMEM)
    return pl.pallas_call(
        kernel,
        out_shape=outs,
        in_specs=[smem] * len(scalars) + [vmem] * len(args),
        out_specs=jax.tree.map(lambda _: vmem, outs),
        scratch_shapes=scratch,
        compiler_params=pltpu.CompilerParams(vmem_limit_bytes=VMEM_LIMIT),
        cost_estimate=pl.CostEstimate(flops=flops, bytes_accessed=moved, transcendentals=0),
    )(*scalars, *args)


def swap(value, axis, bit):
    return lax.ppermute(value, axis, [(i, i ^ bit) for i in range(lax.axis_size(axis))])


def local(field, start):
    spec_count, rows, cols_y, cells_z = field.shape
    n = lax.axis_index("narrow")
    core = n % 2
    chip = n // 2
    wide = lax.axis_size("wide")
    count = spec_count * cols_y * cells_z * wide
    where = n.reshape(1).astype(jnp.int32)
    shape = jax.ShapeDtypeStruct

    def species(k):
        return jnp.swapaxes(lax.dynamic_index_in_dim(field, n ^ k, 0, keepdims=False), 0, 1)

    f0, f1, f2, f3 = (species(k) for k in range(4))
    far2 = swap(f2, "narrow", 2)
    near0 = swap(f1, "narrow", 1)
    near2 = swap(f3, "narrow", 1)

    half = 2 * rows
    block = shape((half, half), F32)
    acc = pltpu.VMEM((half, half), F32)
    same = call(
        same_kernel, block, [acc, acc], [where], [f0, f2, near0, near2],
        100 * half * half * 2 * cols_y * cells_z, 8 * rows * cols_y * cells_z * 4,
    )
    steps = [("wide", 1), ("wide", 2), ("wide", 8), ("wide", 16)]

    def place(axis, bit):
        index = core if axis == "narrow" else lax.axis_index("wide") // bit
        return index % 2

    part = same
    path = [("narrow", 1)] + steps
    for axis, bit in path:
        size = part.shape[0] // 2
        mine = place(axis, bit)
        keep = lax.dynamic_slice_in_dim(part, mine * size, size)
        part = keep + swap(lax.dynamic_slice_in_dim(part, (1 - mine) * size, size), axis, bit)
    group = lax.axis_size("narrow")
    across = [(i, i ^ 2 ^ (4 * group)) for i in range(wide * group)]
    peer = swap(part, "narrow", 2)
    twin = swap(part, "wide", 4)
    peer_twin = lax.ppermute(part, ("wide", "narrow"), across)
    peer, twin, peer_twin, far2, f3 = lax.optimization_barrier((peer, twin, peer_twin, far2, f3))
    twin = part + twin
    peer = peer + peer_twin
    both = jnp.stack([twin, peer])
    far3 = swap(f3, "narrow", 3)
    for axis, bit in path[::-1]:
        other = swap(both, axis, bit)
        low = place(axis, bit) == 0
        both = jnp.concatenate([jnp.where(low, both, other), jnp.where(low, other, both)], axis=1)
    both, far3 = lax.optimization_barrier((both, far3))
    g00 = jnp.where(chip == 0, both[0], both[1])
    g11 = jnp.where(chip == 0, both[1], both[0])

    mixed = call(
        other_kernel, block, [acc, acc], [where], [f0, near0, far2, far3],
        2 * 3 * half * half * cols_y * cells_z, 8 * rows * cols_y * cells_z * 4,
    )
    keep = lax.dynamic_slice_in_dim(mixed, core * rows, rows)
    part = keep + swap(lax.dynamic_slice_in_dim(mixed, (1 - core) * rows, rows), "narrow", 1)
    part = part + swap(part, "narrow", 2)
    for axis, bit in [("wide", 4)] + steps:
        part = part + swap(part, axis, bit)
    other = swap(part, "narrow", 1)
    g01 = jnp.concatenate([jnp.where(core == 0, part, other), jnp.where(core == 0, other, part)], axis=0)

    nx, rank = start.shape
    iterate = lambda *refs: iterate_kernel(count, *refs)
    basis, turned = call(
        iterate, (shape((nx, rank), F32), shape((rank, nx), F32)), [pltpu.VMEM((nx, nx), F32), pltpu.VMEM((rank, 2 * rank), F32)],
        [], [g00, g11, g01, start], 2 * 6 * 3 * nx * nx * rank, 4 * nx * nx,
    )

    share = rank // 4

    def project(ranks, turned):
        piece = shape((cols_y, share, cells_z), F32)
        return call(
            lambda *refs: project_kernel(ranks, *refs), (piece, piece),
            [],
            [where], [turned, f0, near0, far2, far3],
            2 * 3 * 2 * share * nx * cols_y * cells_z, nx * cols_y * cells_z * 4,
        )

    to2, to3 = project((2, 3), turned)
    to2, to3, held = lax.optimization_barrier((to2, to3, turned))
    from2 = swap(to2, "narrow", 2)
    from3 = swap(to3, "narrow", 3)
    mine, to1 = project((0, 1), held)
    from1 = swap(to1, "narrow", 1)
    core_out = jnp.zeros((share, spec_count, cols_y, cells_z), F32)
    for k, piece in enumerate((mine, from1, from2, from3)):
        core_out = lax.dynamic_update_slice_in_dim(core_out, jnp.swapaxes(piece, 0, 1)[:, None], n ^ k, axis=1)
    return (basis, core_out)


def solution(mesh):
    return jax.shard_map(
        local,
        mesh=mesh,
        in_specs=(P(None, "narrow", "wide", None), P()),
        out_specs=(P(), P("narrow", None, "wide", None)),
        check_vma=False,
    )
```

```python
import jax
import jax.numpy as jnp
from jax import lax
from jax.experimental import pallas as pl
from jax.experimental.layout import Layout, with_layout_constraint
from jax.experimental.pallas import tpu as pltpu
from jax.sharding import PartitionSpec as P

ITERS = 3
HIGHEST = lax.Precision.HIGHEST
F32 = jnp.float32
BF16 = jnp.bfloat16
VMEM_LIMIT = 24 * 1024 * 1024


def contract_lanes(a, b):
    return lax.dot_general(a, b, (((1,), (1,)), ((), ())), preferred_element_type=F32)


def split(value):
    hi = value.astype(BF16)
    return hi, (value - hi.astype(F32)).astype(BF16)


def pair(first, second):
    return split(jnp.concatenate([first, second], axis=0))


def store_in_order(keep, send, total, swapped, turned):
    half = total.shape[0] // 2
    for core in (0, 1):
        for turn in (0, 1):

            @pl.when((swapped == core) & (turned == turn))
            def _(core=core, turn=turn):
                value = total.T if turn else total
                for out, rows in ((keep, value[:half]), (send, value[half:])):
                    if core:
                        out[:, :half] = rows[:, half:]
                        out[:, half:] = rows[:, :half]
                    else:
                        out[...] = rows


def same_kernel(where, own0, own2, near0, near2, keep, send, main, cross):
    main[...] = jnp.zeros_like(main)
    cross[...] = jnp.zeros_like(cross)
    for own, near in ((own0, near0), (own2, near2)):
        for y in range(own.shape[0]):
            hi, lo = pair(own[y], near[y])
            main[...] += contract_lanes(hi, hi)
            cross[...] += contract_lanes(hi, lo)
    store_in_order(keep, send, main[...] + cross[...] + cross[...].T, where[0] % 2, 0)


def block_kernel(own, near, far, out, main, cross):
    main[...] = jnp.zeros_like(main)
    cross[...] = jnp.zeros_like(cross)
    for y in range(far.shape[0]):
        hi, lo = pair(own[y], near[y])
        far_hi, far_lo = split(far[y])
        main[...] += contract_lanes(hi, far_hi)
        cross[...] += contract_lanes(hi, far_lo)
        cross[...] += contract_lanes(lo, far_hi)
    out[...] = main[...] + cross[...]


def other_kernel(where, own, near, far3, block2, keep, send, main, cross):
    block_kernel(own, near, far3, main, main, cross)
    total = jnp.concatenate([block2[...], main[...]], axis=1)
    store_in_order(keep, send, total, where[0] % 2, where[0] // 2)


def panel(rows, inverse, block):
    shape = rows.shape
    sub = lax.broadcasted_iota(jnp.int32, shape, 0)
    cols = [jnp.broadcast_to(rows[:, 8 * block + m : 8 * block + m + 1], shape) for m in range(8)]
    pivots = jnp.ones(shape, F32)
    for j in range(8):
        pivot = jnp.broadcast_to(cols[j][j : j + 1], shape)
        pivots = jnp.where(sub == j, pivot, pivots)
        if j < 7:
            factor = jnp.where(sub > j, cols[j] / pivot, 0.0)
            for m in range(j + 1, 8):
                cols[m] = cols[m] - factor * jnp.broadcast_to(cols[m][j : j + 1], shape)
            rows = rows - factor * jnp.broadcast_to(rows[j : j + 1], shape)
            inverse = inverse - factor * jnp.broadcast_to(inverse[j : j + 1], shape)
    scale = lax.rsqrt(pivots)
    return rows * scale, inverse * scale


def inverse_factor(cross, work):
    rank = cross.shape[0]
    row = lax.broadcasted_iota(jnp.int32, cross.shape, 0)
    col = lax.broadcasted_iota(jnp.int32, cross.shape, 1)
    work[:, :rank] = cross
    work[:, rank:] = jnp.where(row == col, 1.0, 0.0)
    for block in range(rank // 8):
        at = pl.ds(8 * block, 8)
        upper, inverse = panel(work[at, :rank], work[at, rank:], block)
        work[at, rank:] = inverse
        after = 8 * block + 8
        if after < rank:
            both = jnp.concatenate([upper, inverse], axis=1)
            update = lax.dot_general(
                upper, both, (((0,), (0,)), ((), ())), precision=HIGHEST, preferred_element_type=F32
            )
            work[after:, :] -= update[after:]
    return work[:, rank:]


def iterate_kernel(count, g00, g11, g01, start, basis, turned, gram, work):
    half = g00.shape[0]
    scale = 1.0 / count
    gram[:half, :half] = g00[...] * scale
    gram[half:, half:] = g11[...] * scale
    gram[:half, half:] = g01[...] * scale
    gram[half:, :half] = g01[...].T * scale
    now = start[...]
    for _ in range(ITERS):
        product = jnp.dot(gram[...], now, precision=HIGHEST, preferred_element_type=F32)
        cross = lax.dot_general(
            product, product, (((0,), (0,)), ((), ())), precision=HIGHEST, preferred_element_type=F32
        )
        inverse = inverse_factor(cross, work)
        now = lax.dot_general(
            product, inverse, (((1,), (1,)), ((), ())), precision=HIGHEST, preferred_element_type=F32
        )
    basis[...] = now
    turned[...] = now.T


def project_kernel(where, turned, own, near, far2, far3, *outs):
    here = where[0]
    cells_y, rows, _ = own.shape
    share = turned.shape[0] // len(outs)
    lines = []
    for rank in range(len(outs)):
        line = pl.ds(pl.multiple_of((here ^ rank) * share, share), share)
        cols = [turned[line, pl.ds(pl.multiple_of((here ^ k) * rows, rows), rows)] for k in range(4)]
        lines.append(jnp.concatenate(cols, axis=1))
    b_hi, b_lo = split(jnp.concatenate(lines, axis=0))
    b_both = jnp.concatenate([b_hi, b_lo], axis=0)
    rank = turned.shape[0]
    for y in range(cells_y):
        f_hi, f_lo = split(jnp.concatenate([own[y], near[y], far2[y], far3[y]], axis=0))
        with_hi = jnp.dot(b_both, f_hi, preferred_element_type=F32)
        with_lo = jnp.dot(b_hi, f_lo, preferred_element_type=F32)
        total = with_hi[:rank] + with_hi[rank:] + with_lo
        for i, out in enumerate(outs):
            out[y] = total[share * i : share * (i + 1)]


def call(kernel, outs, scratch, scalars, args, flops, moved):
    smem = pl.BlockSpec(memory_space=pltpu.SMEM)
    vmem = pl.BlockSpec(memory_space=pltpu.VMEM)
    return pl.pallas_call(
        kernel,
        out_shape=outs,
        in_specs=[smem] * len(scalars) + [vmem] * len(args),
        out_specs=jax.tree.map(lambda _: vmem, outs),
        scratch_shapes=scratch,
        compiler_params=pltpu.CompilerParams(vmem_limit_bytes=VMEM_LIMIT),
        cost_estimate=pl.CostEstimate(flops=flops, bytes_accessed=moved, transcendentals=0),
    )(*scalars, *args)


def as_it_lies(value):
    return with_layout_constraint(value, Layout(major_to_minor=tuple(range(value.ndim))))


def swap(value, axis, bit):
    return lax.ppermute(value, axis, [(i, i ^ bit) for i in range(lax.axis_size(axis))])


def local(field, start):
    spec_count, rows, cols_y, cells_z = field.shape
    n = lax.axis_index("narrow")
    core = n % 2
    chip = n // 2
    wide = lax.axis_size("wide")
    count = spec_count * cols_y * cells_z * wide
    where = n.reshape(1).astype(jnp.int32)
    shape = jax.ShapeDtypeStruct

    def species(array, k):
        return lax.dynamic_index_in_dim(array, n ^ k, 0, keepdims=False)

    def by_y(array):
        return jnp.swapaxes(array, 0, 1)

    f2 = by_y(species(field, 2))
    far2 = swap(f2, "narrow", 2)
    rest, f2 = lax.optimization_barrier((field, f2))
    f0, f1, f3 = (species(rest, k) for k in (0, 1, 3))
    near0 = by_y(as_it_lies(swap(as_it_lies(f1), "narrow", 1)))
    near2 = by_y(as_it_lies(swap(as_it_lies(f3), "narrow", 1)))
    f0 = by_y(f0)
    f3 = by_y(f3)

    half = 2 * rows
    strip = shape((rows, half), F32)
    acc2 = pltpu.VMEM((half, rows), F32)
    acc = pltpu.VMEM((half, half), F32)
    keep, send = call(
        same_kernel, (strip, strip), [acc, acc], [where], [f0, f2, near0, near2],
        2 * 2 * half * half * 2 * cols_y * cells_z, 8 * rows * cols_y * cells_z * 4,
    )
    steps = [("wide", 1), ("wide", 2), ("wide", 8), ("wide", 16)]

    def place(axis, bit):
        index = core if axis == "narrow" else lax.axis_index("wide") // bit
        return index % 2

    path = [("narrow", 1)] + steps
    part = keep + swap(send, "narrow", 1)
    for axis, bit in steps:
        size = part.shape[0] // 2
        mine = place(axis, bit)
        keep = lax.dynamic_slice_in_dim(part, mine * size, size)
        part = keep + swap(lax.dynamic_slice_in_dim(part, (1 - mine) * size, size), axis, bit)
    group = lax.axis_size("narrow")
    across = [(i, i ^ 2 ^ (4 * group)) for i in range(wide * group)]
    peer = swap(part, "narrow", 2)
    twin = swap(part, "wide", 4)
    peer_twin = lax.ppermute(part, ("wide", "narrow"), across)
    peer, twin, peer_twin, far2, f3 = lax.optimization_barrier((peer, twin, peer_twin, far2, f3))
    twin = part + twin
    peer = peer + peer_twin
    both = jnp.stack([twin, peer])
    far3 = swap(f3, "narrow", 3)
    for axis, bit in path[::-1]:
        other = swap(both, axis, bit)
        low = place(axis, bit) == 0
        both = jnp.concatenate([jnp.where(low, both, other), jnp.where(low, other, both)], axis=1)
    both, far3 = lax.optimization_barrier((both, far3))
    g00 = jnp.where(chip == 0, both[0], both[1])
    g11 = jnp.where(chip == 0, both[1], both[0])

    block2 = call(
        block_kernel, shape((half, rows), F32), [acc2, acc2], [], [f0, near0, far2],
        2 * 3 * half * rows * cols_y * cells_z, 6 * rows * cols_y * cells_z * 4,
    )
    block2, far3 = lax.optimization_barrier((block2, far3))
    keep, send = call(
        other_kernel, (strip, strip), [acc2, acc2], [where], [f0, near0, far3, block2],
        2 * 3 * half * rows * cols_y * cells_z, 6 * rows * cols_y * cells_z * 4,
    )
    part = keep + swap(send, "narrow", 1)
    part = part + swap(part, "narrow", 2)
    for axis, bit in [("wide", 4)] + steps:
        part = part + swap(part, axis, bit)
    other = swap(part, "narrow", 1)
    g01 = jnp.concatenate([jnp.where(core == 0, part, other), jnp.where(core == 0, other, part)], axis=0)

    nx, rank = start.shape
    iterate = lambda *refs: iterate_kernel(count, *refs)
    basis, turned = call(
        iterate, (shape((nx, rank), F32), shape((rank, nx), F32)), [pltpu.VMEM((nx, nx), F32), pltpu.VMEM((rank, 2 * rank), F32)],
        [], [g00, g11, g01, start], 2 * 6 * 3 * nx * nx * rank, 4 * nx * nx,
    )

    share = rank // 4
    piece = shape((cols_y, share, cells_z), F32)
    mine, to1, to2, to3 = call(
        project_kernel, (piece,) * 4, [], [where], [turned, f0, near0, far2, far3],
        2 * 3 * rank * nx * cols_y * cells_z, nx * cols_y * cells_z * 4,
    )
    from2 = swap(to2, "narrow", 2)
    from3 = swap(to3, "narrow", 3)
    from1 = swap(to1, "narrow", 1)
    core_out = jnp.zeros((share, spec_count, cols_y, cells_z), F32)
    for k, piece in enumerate((mine, from1, from2, from3)):
        core_out = lax.dynamic_update_slice_in_dim(core_out, jnp.swapaxes(piece, 0, 1)[:, None], n ^ k, axis=1)
    return (basis, core_out)


def solution(mesh):
    return jax.shard_map(
        local,
        mesh=mesh,
        in_specs=(P(None, "narrow", "wide", None), P()),
        out_specs=(P(), P("narrow", None, "wide", None)),
        check_vma=False,
    )
```

```python
import jax
import jax.numpy as jnp
from jax import lax
from jax.experimental import pallas as pl
from jax.experimental.layout import Layout, with_layout_constraint
from jax.experimental.pallas import tpu as pltpu
from jax.sharding import PartitionSpec as P

ITERS = 3
HIGHEST = lax.Precision.HIGHEST
F32 = jnp.float32
BF16 = jnp.bfloat16
VMEM_LIMIT = 24 * 1024 * 1024


def contract_lanes(a, b):
    return lax.dot_general(a, b, (((1,), (1,)), ((), ())), preferred_element_type=F32)


def split(value):
    hi = value.astype(BF16)
    return hi, (value - hi.astype(F32)).astype(BF16)


def pair(first, second):
    return split(jnp.concatenate([first, second], axis=0))


def store_in_order(keep, send, total, swapped, turned):
    half = total.shape[0] // 2
    for core in (0, 1):
        for turn in (0, 1):

            @pl.when((swapped == core) & (turned == turn))
            def _(core=core, turn=turn):
                value = total.T if turn else total
                for out, rows in ((keep, value[:half]), (send, value[half:])):
                    if core:
                        out[:, :half] = rows[:, half:]
                        out[:, half:] = rows[:, :half]
                    else:
                        out[...] = rows


def same_kernel(where, own0, own2, near0, near2, keep, send, main, cross):
    main[...] = jnp.zeros_like(main)
    cross[...] = jnp.zeros_like(cross)
    for own, near in ((own0, near0), (own2, near2)):
        for y in range(own.shape[0]):
            hi, lo = pair(own[y], near[y])
            main[...] += contract_lanes(hi, hi)
            cross[...] += contract_lanes(hi, lo)
    store_in_order(keep, send, main[...] + cross[...] + cross[...].T, where[0] % 2, 0)


def block_kernel(own, near, far, out, main, cross):
    main[...] = jnp.zeros_like(main)
    cross[...] = jnp.zeros_like(cross)
    for y in range(far.shape[0]):
        hi, lo = pair(own[y], near[y])
        far_hi, far_lo = split(far[y])
        main[...] += contract_lanes(hi, far_hi)
        cross[...] += contract_lanes(hi, far_lo)
        cross[...] += contract_lanes(lo, far_hi)
    out[...] = main[...] + cross[...]


def other_kernel(where, own, near, far3, block2, keep, send, main, cross):
    block_kernel(own, near, far3, main, main, cross)
    total = jnp.concatenate([block2[...], main[...]], axis=1)
    store_in_order(keep, send, total, where[0] % 2, where[0] // 2)


PANEL = 32


def panel(rows, inverse, base):
    count = len(rows)
    shape = rows[0].shape
    sub = lax.broadcasted_iota(jnp.int32, shape, 0)
    size = 8 * count
    cols = [[jnp.broadcast_to(block[:, base + m : base + m + 1], shape) for block in rows] for m in range(size)]
    pivots = [jnp.ones(shape, F32) for _ in range(count)]

    def line(block, row):
        return jnp.broadcast_to(block[row : row + 1], shape)

    for j in range(size):
        at, row = divmod(j, 8)
        pivot = line(cols[j][at], row)
        pivots[at] = jnp.where(sub == row, pivot, pivots[at])
        if j == size - 1:
            break
        reciprocal = 1.0 / pivot
        row_line, inverse_line = line(rows[at], row), line(inverse[at], row)
        col_lines = {m: line(cols[m][at], row) for m in range(j + 1, size)}
        for b in range((j + 1) // 8, count):
            factor = cols[j][b] * reciprocal
            if b == at:
                factor = jnp.where(sub > row, factor, 0.0)
            for m in range(j + 1, size):
                cols[m][b] = cols[m][b] - factor * col_lines[m]
            rows[b] = rows[b] - factor * row_line
            inverse[b] = inverse[b] - factor * inverse_line
    scales = [lax.rsqrt(p) for p in pivots]
    joined = lambda blocks: jnp.concatenate([b * s for b, s in zip(blocks, scales)], axis=0)
    return joined(rows), joined(inverse)


def inverse_factor(cross, work):
    rank = cross.shape[0]
    row = lax.broadcasted_iota(jnp.int32, cross.shape, 0)
    col = lax.broadcasted_iota(jnp.int32, cross.shape, 1)
    work[:, :rank] = cross
    work[:, rank:] = jnp.where(row == col, 1.0, 0.0)
    for base in range(0, rank, PANEL):
        starts = range(base, base + PANEL, 8)
        upper, inverse = panel([work[i : i + 8, :rank] for i in starts], [work[i : i + 8, rank:] for i in starts], base)
        after = base + PANEL
        work[base:after, rank:] = inverse
        if after < rank:
            both = jnp.concatenate([upper, inverse], axis=1)
            work[after:, :] -= lax.dot_general(
                upper[:, after:], both, (((0,), (0,)), ((), ())), precision=HIGHEST, preferred_element_type=F32
            )
    return work[:, rank:]


def split3(value):
    first = value.astype(BF16)
    rest = value - first.astype(F32)
    second = rest.astype(BF16)
    return first, second, (rest - second.astype(F32)).astype(BF16)


def iterate_kernel(count, g00, g11, g01, start, basis, turned, pieces, work):
    nx, rank = start.shape
    half = nx // 2
    scale = 1.0 / count
    blocks = ((0, 0, g00[...]), (1, 1, g11[...]), (0, 1, g01[...]), (1, 0, g01[...].T))
    for i, j, block in blocks:
        for k, piece in enumerate(split3(block * scale)):
            row = k * nx + i * half
            pieces[row : row + half, j * half : (j + 1) * half] = piece
    now = start[...]
    for _ in range(ITERS):
        n0, n1, n2 = split3(now)
        wide = jnp.dot(pieces[...], jnp.concatenate([n0, n1], axis=1), preferred_element_type=F32)
        small = jnp.dot(pieces[:nx], n2, preferred_element_type=F32) + wide[nx : 2 * nx, rank:] + wide[2 * nx :, :rank]
        product = wide[:nx, :rank] + ((wide[:nx, rank:] + wide[nx : 2 * nx, :rank]) + small)
        cross = lax.dot_general(
            product, product, (((0,), (0,)), ((), ())), precision=HIGHEST, preferred_element_type=F32
        )
        inverse = inverse_factor(cross, work)
        now = lax.dot_general(
            product, inverse, (((1,), (1,)), ((), ())), precision=HIGHEST, preferred_element_type=F32
        )
    basis[...] = now
    turned[...] = now.T


def project_kernel(where, turned, own, near, far2, far3, *outs):
    here = where[0]
    cells_y, rows, _ = own.shape
    share = turned.shape[0] // len(outs)
    lines = []
    for rank in range(len(outs)):
        line = pl.ds(pl.multiple_of((here ^ rank) * share, share), share)
        cols = [turned[line, pl.ds(pl.multiple_of((here ^ k) * rows, rows), rows)] for k in range(4)]
        lines.append(jnp.concatenate(cols, axis=1))
    b_hi, b_lo = split(jnp.concatenate(lines, axis=0))
    b_both = jnp.concatenate([b_hi, b_lo], axis=0)
    rank = turned.shape[0]
    for y in range(cells_y):
        f_hi, f_lo = split(jnp.concatenate([own[y], near[y], far2[y], far3[y]], axis=0))
        with_hi = jnp.dot(b_both, f_hi, preferred_element_type=F32)
        with_lo = jnp.dot(b_hi, f_lo, preferred_element_type=F32)
        total = with_hi[:rank] + with_hi[rank:] + with_lo
        for i, out in enumerate(outs):
            out[y] = total[share * i : share * (i + 1)]


def call(kernel, outs, scratch, scalars, args, flops, moved):
    smem = pl.BlockSpec(memory_space=pltpu.SMEM)
    vmem = pl.BlockSpec(memory_space=pltpu.VMEM)
    return pl.pallas_call(
        kernel,
        out_shape=outs,
        in_specs=[smem] * len(scalars) + [vmem] * len(args),
        out_specs=jax.tree.map(lambda _: vmem, outs),
        scratch_shapes=scratch,
        compiler_params=pltpu.CompilerParams(vmem_limit_bytes=VMEM_LIMIT),
        cost_estimate=pl.CostEstimate(flops=flops, bytes_accessed=moved, transcendentals=0),
    )(*scalars, *args)


def as_it_lies(value):
    return with_layout_constraint(value, Layout(major_to_minor=tuple(range(value.ndim))))


def swap(value, axis, bit):
    return lax.ppermute(value, axis, [(i, i ^ bit) for i in range(lax.axis_size(axis))])


def local(field, start):
    spec_count, rows, cols_y, cells_z = field.shape
    n = lax.axis_index("narrow")
    core = n % 2
    chip = n // 2
    wide = lax.axis_size("wide")
    count = spec_count * cols_y * cells_z * wide
    where = n.reshape(1).astype(jnp.int32)
    shape = jax.ShapeDtypeStruct

    def species(array, k):
        return lax.dynamic_index_in_dim(array, n ^ k, 0, keepdims=False)

    def by_y(array):
        return jnp.swapaxes(array, 0, 1)

    f2 = by_y(species(field, 2))
    far2 = swap(f2, "narrow", 2)
    rest, f2 = lax.optimization_barrier((field, f2))
    f0, f1, f3 = (species(rest, k) for k in (0, 1, 3))
    near0 = by_y(as_it_lies(swap(as_it_lies(f1), "narrow", 1)))
    near2 = by_y(as_it_lies(swap(as_it_lies(f3), "narrow", 1)))
    f0 = by_y(f0)
    f3 = by_y(f3)

    half = 2 * rows
    strip = shape((rows, half), F32)
    acc2 = pltpu.VMEM((half, rows), F32)
    acc = pltpu.VMEM((half, half), F32)
    keep, send = call(
        same_kernel, (strip, strip), [acc, acc], [where], [f0, f2, near0, near2],
        2 * 2 * half * half * 2 * cols_y * cells_z, 8 * rows * cols_y * cells_z * 4,
    )
    steps = [("wide", 1), ("wide", 2), ("wide", 8), ("wide", 16)]

    def place(axis, bit):
        index = core if axis == "narrow" else lax.axis_index("wide") // bit
        return index % 2

    path = [("narrow", 1)] + steps
    part = keep + swap(send, "narrow", 1)
    for axis, bit in steps:
        size = part.shape[0] // 2
        mine = place(axis, bit)
        keep = lax.dynamic_slice_in_dim(part, mine * size, size)
        part = keep + swap(lax.dynamic_slice_in_dim(part, (1 - mine) * size, size), axis, bit)
    group = lax.axis_size("narrow")
    across = [(i, i ^ 2 ^ (4 * group)) for i in range(wide * group)]
    peer = swap(part, "narrow", 2)
    twin = swap(part, "wide", 4)
    peer_twin = lax.ppermute(part, ("wide", "narrow"), across)
    peer, twin, peer_twin, far2, f3 = lax.optimization_barrier((peer, twin, peer_twin, far2, f3))
    twin = part + twin
    peer = peer + peer_twin
    both = jnp.stack([twin, peer])
    far3 = swap(f3, "narrow", 3)
    for axis, bit in path[::-1]:
        other = swap(both, axis, bit)
        low = place(axis, bit) == 0
        both = jnp.concatenate([jnp.where(low, both, other), jnp.where(low, other, both)], axis=1)
    both, far3 = lax.optimization_barrier((both, far3))
    g00 = jnp.where(chip == 0, both[0], both[1])
    g11 = jnp.where(chip == 0, both[1], both[0])

    block2 = call(
        block_kernel, shape((half, rows), F32), [acc2, acc2], [], [f0, near0, far2],
        2 * 3 * half * rows * cols_y * cells_z, 6 * rows * cols_y * cells_z * 4,
    )
    block2, far3 = lax.optimization_barrier((block2, far3))
    keep, send = call(
        other_kernel, (strip, strip), [acc2, acc2], [where], [f0, near0, far3, block2],
        2 * 3 * half * rows * cols_y * cells_z, 6 * rows * cols_y * cells_z * 4,
    )
    part = keep + swap(send, "narrow", 1)
    part = part + swap(part, "narrow", 2)
    for axis, bit in [("wide", 4)] + steps:
        part = part + swap(part, axis, bit)
    other = swap(part, "narrow", 1)
    g01 = jnp.concatenate([jnp.where(core == 0, part, other), jnp.where(core == 0, other, part)], axis=0)

    nx, rank = start.shape
    iterate = lambda *refs: iterate_kernel(count, *refs)
    basis, turned = call(
        iterate, (shape((nx, rank), F32), shape((rank, nx), F32)), [pltpu.VMEM((3 * nx, nx), BF16), pltpu.VMEM((rank, 2 * rank), F32)],
        [], [g00, g11, g01, start], 2 * 6 * 3 * nx * nx * rank, 4 * nx * nx,
    )

    share = rank // 4
    piece = shape((cols_y, share, cells_z), F32)
    mine, to1, to2, to3 = call(
        project_kernel, (piece,) * 4, [], [where], [turned, f0, near0, far2, far3],
        2 * 3 * rank * nx * cols_y * cells_z, nx * cols_y * cells_z * 4,
    )
    from2 = swap(to2, "narrow", 2)
    from3 = swap(to3, "narrow", 3)
    from1 = swap(to1, "narrow", 1)
    core_out = jnp.zeros((share, spec_count, cols_y, cells_z), F32)
    for k, piece in enumerate((mine, from1, from2, from3)):
        core_out = lax.dynamic_update_slice_in_dim(core_out, jnp.swapaxes(piece, 0, 1)[:, None], n ^ k, axis=1)
    return (basis, core_out)


def solution(mesh):
    return jax.shard_map(
        local,
        mesh=mesh,
        in_specs=(P(None, "narrow", "wide", None), P()),
        out_specs=(P(), P("narrow", None, "wide", None)),
        check_vma=False,
    )
```

```python
import jax
import jax.numpy as jnp
from jax import lax
from jax.experimental import pallas as pl
from jax.experimental.layout import Layout, with_layout_constraint
from jax.experimental.pallas import tpu as pltpu
from jax.sharding import PartitionSpec as P

ITERS = 3
HIGHEST = lax.Precision.HIGHEST
F32 = jnp.float32
BF16 = jnp.bfloat16
VMEM_LIMIT = 24 * 1024 * 1024


def contract_lanes(a, b):
    return lax.dot_general(a, b, (((1,), (1,)), ((), ())), preferred_element_type=F32)


def split(value):
    hi = value.astype(BF16)
    return hi, (value - hi.astype(F32)).astype(BF16)


def pair(first, second):
    return split(jnp.concatenate([first, second], axis=0))


def store_in_order(keep, send, total, swapped, turned):
    half = total.shape[0] // 2
    for core in (0, 1):
        for turn in (0, 1):

            @pl.when((swapped == core) & (turned == turn))
            def _(core=core, turn=turn):
                value = total.T if turn else total
                for out, rows in ((keep, value[:half]), (send, value[half:])):
                    if core:
                        out[:, :half] = rows[:, half:]
                        out[:, half:] = rows[:, :half]
                    else:
                        out[...] = rows


def same_kernel(where, own0, own2, near0, near2, keep, send, main, cross):
    main[...] = jnp.zeros_like(main)
    cross[...] = jnp.zeros_like(cross)
    for own, near in ((own0, near0), (own2, near2)):
        for y in range(own.shape[0]):
            hi, lo = pair(own[y], near[y])
            main[...] += contract_lanes(hi, hi)
            cross[...] += contract_lanes(hi, lo)
    store_in_order(keep, send, main[...] + cross[...] + cross[...].T, where[0] % 2, 0)


def block_kernel(own, near, far, out, main, cross):
    main[...] = jnp.zeros_like(main)
    cross[...] = jnp.zeros_like(cross)
    for y in range(far.shape[0]):
        hi, lo = pair(own[y], near[y])
        far_hi, far_lo = split(far[y])
        main[...] += contract_lanes(hi, far_hi)
        cross[...] += contract_lanes(hi, far_lo)
        cross[...] += contract_lanes(lo, far_hi)
    out[...] = main[...] + cross[...]


def other_kernel(where, own, near, far3, block2, keep, send, main, cross):
    block_kernel(own, near, far3, main, main, cross)
    total = jnp.concatenate([block2[...], main[...]], axis=1)
    store_in_order(keep, send, total, where[0] % 2, where[0] // 2)


PANEL = 32


def panel(rows, inverse, base):
    count = len(rows)
    shape = rows[0].shape
    sub = lax.broadcasted_iota(jnp.int32, shape, 0)
    size = 8 * count
    cols = [[jnp.broadcast_to(block[:, base + m : base + m + 1], shape) for block in rows] for m in range(size)]
    pivots = [jnp.ones(shape, F32) for _ in range(count)]

    def line(block, row):
        return jnp.broadcast_to(block[row : row + 1], shape)

    for j in range(size):
        at, row = divmod(j, 8)
        pivot = line(cols[j][at], row)
        pivots[at] = jnp.where(sub == row, pivot, pivots[at])
        if j == size - 1:
            break
        reciprocal = 1.0 / pivot
        row_line, inverse_line = line(rows[at], row), line(inverse[at], row)
        col_lines = {m: line(cols[m][at], row) for m in range(j + 1, size)}
        for b in range((j + 1) // 8, count):
            factor = cols[j][b] * reciprocal
            if b == at:
                factor = jnp.where(sub > row, factor, 0.0)
            for m in range(j + 1, size):
                cols[m][b] = cols[m][b] - factor * col_lines[m]
            rows[b] = rows[b] - factor * row_line
            inverse[b] = inverse[b] - factor * inverse_line
    scales = [lax.rsqrt(p) for p in pivots]
    joined = lambda blocks: jnp.concatenate([b * s for b, s in zip(blocks, scales)], axis=0)
    return joined(rows), joined(inverse)


def inverse_factor(cross, work):
    rank = cross.shape[0]
    row = lax.broadcasted_iota(jnp.int32, cross.shape, 0)
    col = lax.broadcasted_iota(jnp.int32, cross.shape, 1)
    work[:, :rank] = cross
    work[:, rank:] = jnp.where(row == col, 1.0, 0.0)
    for base in range(0, rank, PANEL):
        starts = range(base, base + PANEL, 8)
        upper, inverse = panel([work[i : i + 8, :rank] for i in starts], [work[i : i + 8, rank:] for i in starts], base)
        after = base + PANEL
        work[base:after, rank:] = inverse
        if after < rank:
            both = jnp.concatenate([upper, inverse], axis=1)
            work[after:, :] -= lax.dot_general(
                upper[:, after:], both, (((0,), (0,)), ((), ())), precision=HIGHEST, preferred_element_type=F32
            )
    return work[:, rank:]


def split3(value):
    first = value.astype(BF16)
    rest = value - first.astype(F32)
    second = rest.astype(BF16)
    return first, second, (rest - second.astype(F32)).astype(BF16)


def iterate_kernel(count, g00, g11, g01, start, basis, turned, pieces, work):
    nx, rank = start.shape
    half = nx // 2
    scale = 1.0 / count
    blocks = ((0, 0, g00[...]), (1, 1, g11[...]), (0, 1, g01[...]), (1, 0, g01[...].T))
    for i, j, block in blocks:
        for k, piece in enumerate(split3(block * scale)):
            row = k * nx + i * half
            pieces[row : row + half, j * half : (j + 1) * half] = piece
    now = start[...]
    for _ in range(ITERS):
        n0, n1, n2 = split3(now)
        wide = jnp.dot(pieces[...], jnp.concatenate([n0, n1], axis=1), preferred_element_type=F32)
        small = jnp.dot(pieces[:nx], n2, preferred_element_type=F32) + wide[nx : 2 * nx, rank:] + wide[2 * nx :, :rank]
        product = wide[:nx, :rank] + ((wide[:nx, rank:] + wide[nx : 2 * nx, :rank]) + small)
        cross = lax.dot_general(
            product, product, (((0,), (0,)), ((), ())), precision=HIGHEST, preferred_element_type=F32
        )
        inverse = inverse_factor(cross, work)
        now = lax.dot_general(
            product, inverse, (((1,), (1,)), ((), ())), precision=HIGHEST, preferred_element_type=F32
        )
    basis[...] = now
    turned[...] = now.T


def project_kernel(where, turned, own, near, far2, far3, *outs):
    here = where[0]
    cells_y, rows, _ = own.shape
    share = turned.shape[0] // len(outs)
    lines = []
    for rank in range(len(outs)):
        line = pl.ds(pl.multiple_of((here ^ rank) * share, share), share)
        cols = [turned[line, pl.ds(pl.multiple_of((here ^ k) * rows, rows), rows)] for k in range(4)]
        lines.append(jnp.concatenate(cols, axis=1))
    b_hi, b_lo = split(jnp.concatenate(lines, axis=0))
    b_both = jnp.concatenate([b_hi, b_lo], axis=0)
    rank = turned.shape[0]
    for y in range(cells_y):
        f_hi, f_lo = split(jnp.concatenate([own[y], near[y], far2[y], far3[y]], axis=0))
        with_hi = jnp.dot(b_both, f_hi, preferred_element_type=F32)
        with_lo = jnp.dot(b_hi, f_lo, preferred_element_type=F32)
        total = with_hi[:rank] + with_hi[rank:] + with_lo
        for i, out in enumerate(outs):
            out[y] = total[share * i : share * (i + 1)]


def call(kernel, outs, scratch, scalars, args, flops, moved):
    smem = pl.BlockSpec(memory_space=pltpu.SMEM)
    vmem = pl.BlockSpec(memory_space=pltpu.VMEM)
    return pl.pallas_call(
        kernel,
        out_shape=outs,
        in_specs=[smem] * len(scalars) + [vmem] * len(args),
        out_specs=jax.tree.map(lambda _: vmem, outs),
        scratch_shapes=scratch,
        compiler_params=pltpu.CompilerParams(vmem_limit_bytes=VMEM_LIMIT),
        cost_estimate=pl.CostEstimate(flops=flops, bytes_accessed=moved, transcendentals=0),
    )(*scalars, *args)


def as_it_lies(value):
    return with_layout_constraint(value, Layout(major_to_minor=tuple(range(value.ndim))))


def swap(value, axis, bit):
    return lax.ppermute(value, axis, [(i, i ^ bit) for i in range(lax.axis_size(axis))])


def local(field, start):
    spec_count, rows, cols_y, cells_z = field.shape
    n = lax.axis_index("narrow")
    core = n % 2
    chip = n // 2
    wide = lax.axis_size("wide")
    count = spec_count * cols_y * cells_z * wide
    where = n.reshape(1).astype(jnp.int32)
    shape = jax.ShapeDtypeStruct

    def species(array, k):
        return lax.dynamic_index_in_dim(array, n ^ k, 0, keepdims=False)

    def by_y(array):
        return jnp.swapaxes(array, 0, 1)

    f2 = by_y(species(field, 2))
    far2 = swap(f2, "narrow", 2)
    rest, f2 = lax.optimization_barrier((field, f2))
    f0, f1, f3 = (species(rest, k) for k in (0, 1, 3))
    near0 = by_y(as_it_lies(swap(as_it_lies(f1), "narrow", 1)))
    near2 = by_y(as_it_lies(swap(as_it_lies(f3), "narrow", 1)))
    f0 = by_y(f0)
    f3 = by_y(f3)

    half = 2 * rows
    strip = shape((rows, half), F32)
    acc2 = pltpu.VMEM((half, rows), F32)
    acc = pltpu.VMEM((half, half), F32)
    keep, send = call(
        same_kernel, (strip, strip), [acc, acc], [where], [f0, f2, near0, near2],
        2 * 2 * half * half * 2 * cols_y * cells_z, 8 * rows * cols_y * cells_z * 4,
    )
    steps = [("wide", 1), ("wide", 2), ("wide", 8), ("wide", 16)]

    def place(axis, bit):
        index = core if axis == "narrow" else lax.axis_index("wide") // bit
        return index % 2

    path = [("narrow", 1)] + steps
    part = keep + swap(send, "narrow", 1)
    for axis, bit in steps:
        size = part.shape[0] // 2
        mine = place(axis, bit)
        keep = lax.dynamic_slice_in_dim(part, mine * size, size)
        part = keep + swap(lax.dynamic_slice_in_dim(part, (1 - mine) * size, size), axis, bit)
    group = lax.axis_size("narrow")
    across = [(i, i ^ 2 ^ (4 * group)) for i in range(wide * group)]
    peer = swap(part, "narrow", 2)
    twin = swap(part, "wide", 4)
    peer_twin = lax.ppermute(part, ("wide", "narrow"), across)
    peer, twin, peer_twin, far2, f3 = lax.optimization_barrier((peer, twin, peer_twin, far2, f3))
    twin = part + twin
    peer = peer + peer_twin
    both = jnp.stack([twin, peer])
    far3 = swap(f3, "narrow", 3)
    for axis, bit in path[::-1]:
        other = swap(both, axis, bit)
        low = place(axis, bit) == 0
        both = jnp.concatenate([jnp.where(low, both, other), jnp.where(low, other, both)], axis=1)
    both, far3 = lax.optimization_barrier((both, far3))
    g00 = jnp.where(chip == 0, both[0], both[1])
    g11 = jnp.where(chip == 0, both[1], both[0])

    block2 = call(
        block_kernel, shape((half, rows), F32), [acc2, acc2], [], [f0, near0, far2],
        2 * 3 * half * rows * cols_y * cells_z, 6 * rows * cols_y * cells_z * 4,
    )
    block2, far3 = lax.optimization_barrier((block2, far3))
    keep, send = call(
        other_kernel, (strip, strip), [acc2, acc2], [where], [f0, near0, far3, block2],
        2 * 3 * half * rows * cols_y * cells_z, 6 * rows * cols_y * cells_z * 4,
    )
    part = keep + swap(send, "narrow", 1)
    size = rows // 2
    held = lax.dynamic_slice_in_dim(part, chip * size, size)
    part = held + swap(lax.dynamic_slice_in_dim(part, (1 - chip) * size, size), "narrow", 2)
    for axis, bit in [("wide", 4)] + steps:
        part = part + swap(part, axis, bit)
    parts = [part, swap(part, "narrow", 1), swap(part, "narrow", 2), swap(part, "narrow", 3)]
    strips = [jnp.where(chip == i, parts[k], parts[k + 2]) for k in (0, 1) for i in (0, 1)]
    g01 = jnp.concatenate([jnp.where(core == 0, strips[i], strips[i ^ 2]) for i in range(4)], axis=0)

    nx, rank = start.shape
    iterate = lambda *refs: iterate_kernel(count, *refs)
    basis, turned = call(
        iterate, (shape((nx, rank), F32), shape((rank, nx), F32)), [pltpu.VMEM((3 * nx, nx), BF16), pltpu.VMEM((rank, 2 * rank), F32)],
        [], [g00, g11, g01, start], 2 * 6 * 3 * nx * nx * rank, 4 * nx * nx,
    )

    share = rank // 4
    piece = shape((cols_y, share, cells_z), F32)
    mine, to1, to2, to3 = call(
        project_kernel, (piece,) * 4, [], [where], [turned, f0, near0, far2, far3],
        2 * 3 * rank * nx * cols_y * cells_z, nx * cols_y * cells_z * 4,
    )
    from2 = swap(to2, "narrow", 2)
    from3 = swap(to3, "narrow", 3)
    from1 = swap(to1, "narrow", 1)
    core_out = jnp.zeros((share, spec_count, cols_y, cells_z), F32)
    for k, piece in enumerate((mine, from1, from2, from3)):
        core_out = lax.dynamic_update_slice_in_dim(core_out, jnp.swapaxes(piece, 0, 1)[:, None], n ^ k, axis=1)
    return (basis, core_out)


def solution(mesh):
    return jax.shard_map(
        local,
        mesh=mesh,
        in_specs=(P(None, "narrow", "wide", None), P()),
        out_specs=(P(), P("narrow", None, "wide", None)),
        check_vma=False,
    )
```

```python
import jax
import jax.numpy as jnp
from jax import lax
from jax.experimental import pallas as pl
from jax.experimental.layout import Layout, with_layout_constraint
from jax.experimental.pallas import tpu as pltpu
from jax.sharding import PartitionSpec as P

ITERS = 3
HIGHEST = lax.Precision.HIGHEST
F32 = jnp.float32
BF16 = jnp.bfloat16
VMEM_LIMIT = 24 * 1024 * 1024


def contract_lanes(a, b):
    return lax.dot_general(a, b, (((1,), (1,)), ((), ())), preferred_element_type=F32)


def split(value):
    hi = value.astype(BF16)
    return hi, (value - hi.astype(F32)).astype(BF16)


def pair(first, second):
    return split(jnp.concatenate([first, second], axis=0))


def store_in_order(keep, send, total, swapped, turned):
    half = total.shape[0] // 2
    for core in (0, 1):
        for turn in (0, 1):

            @pl.when((swapped == core) & (turned == turn))
            def _(core=core, turn=turn):
                value = total.T if turn else total
                for out, rows in ((keep, value[:half]), (send, value[half:])):
                    if core:
                        out[:, :half] = rows[:, half:]
                        out[:, half:] = rows[:, :half]
                    else:
                        out[...] = rows


def same_kernel(where, own0, own2, near0, near2, keep, send, main, cross):
    main[...] = jnp.zeros_like(main)
    cross[...] = jnp.zeros_like(cross)
    for own, near in ((own0, near0), (own2, near2)):
        for y in range(own.shape[0]):
            hi, lo = pair(own[y], near[y])
            main[...] += contract_lanes(hi, hi)
            cross[...] += contract_lanes(hi, lo)
    store_in_order(keep, send, main[...] + cross[...] + cross[...].T, where[0] % 2, 0)


def block_kernel(own, near, far, out, main, cross):
    main[...] = jnp.zeros_like(main)
    cross[...] = jnp.zeros_like(cross)
    for y in range(far.shape[0]):
        hi, lo = pair(own[y], near[y])
        far_hi, far_lo = split(far[y])
        main[...] += contract_lanes(hi, far_hi)
        cross[...] += contract_lanes(hi, far_lo)
        cross[...] += contract_lanes(lo, far_hi)
    out[...] = main[...] + cross[...]


def other_kernel(where, own, near, far3, block2, keep, send, main, cross):
    block_kernel(own, near, far3, main, main, cross)
    total = jnp.concatenate([block2[...], main[...]], axis=1)
    store_in_order(keep, send, total, where[0] % 2, where[0] // 2)


PANEL = 32


def panel(rows, inverse, base):
    count = len(rows)
    shape = rows[0].shape
    sub = lax.broadcasted_iota(jnp.int32, shape, 0)
    size = 8 * count
    cols = [[jnp.broadcast_to(block[:, base + m : base + m + 1], shape) for block in rows] for m in range(size)]
    pivots = [jnp.ones(shape, F32) for _ in range(count)]

    def line(block, row):
        return jnp.broadcast_to(block[row : row + 1], shape)

    for j in range(size):
        at, row = divmod(j, 8)
        pivot = line(cols[j][at], row)
        pivots[at] = jnp.where(sub == row, pivot, pivots[at])
        if j == size - 1:
            break
        reciprocal = 1.0 / pivot
        row_line, inverse_line = line(rows[at], row), line(inverse[at], row)
        col_lines = {m: line(cols[m][at], row) for m in range(j + 1, size)}
        for b in range((j + 1) // 8, count):
            factor = cols[j][b] * reciprocal
            if b == at:
                factor = jnp.where(sub > row, factor, 0.0)
            for m in range(j + 1, size):
                cols[m][b] = cols[m][b] - factor * col_lines[m]
            rows[b] = rows[b] - factor * row_line
            inverse[b] = inverse[b] - factor * inverse_line
    scales = [lax.rsqrt(p) for p in pivots]
    joined = lambda blocks: jnp.concatenate([b * s for b, s in zip(blocks, scales)], axis=0)
    return joined(rows), joined(inverse)


def inverse_factor(cross, work):
    rank = cross.shape[0]
    row = lax.broadcasted_iota(jnp.int32, cross.shape, 0)
    col = lax.broadcasted_iota(jnp.int32, cross.shape, 1)
    work[:, :rank] = cross
    work[:, rank:] = jnp.where(row == col, 1.0, 0.0)
    for base in range(0, rank, PANEL):
        starts = range(base, base + PANEL, 8)
        upper, inverse = panel([work[i : i + 8, :rank] for i in starts], [work[i : i + 8, rank:] for i in starts], base)
        after = base + PANEL
        work[base:after, rank:] = inverse
        if after < rank:
            both = jnp.concatenate([upper, inverse], axis=1)
            work[after:, :] -= lax.dot_general(
                upper[:, after:], both, (((0,), (0,)), ((), ())), precision=HIGHEST, preferred_element_type=F32
            )
    return work[:, rank:]


def split3(value):
    first = value.astype(BF16)
    rest = value - first.astype(F32)
    second = rest.astype(BF16)
    return first, second, (rest - second.astype(F32)).astype(BF16)


def iterate_kernel(count, g00, g11, g01, start, basis, turned, pieces, work):
    nx, rank = start.shape
    half = nx // 2
    scale = 1.0 / count
    blocks = ((0, 0, g00[...]), (1, 1, g11[...]), (0, 1, g01[...]), (1, 0, g01[...].T))
    for i, j, block in blocks:
        for k, piece in enumerate(split3(block * scale)):
            row = k * nx + i * half
            pieces[row : row + half, j * half : (j + 1) * half] = piece
    now = start[...]
    for _ in range(ITERS):
        n0, n1, n2 = split3(now)
        wide = jnp.dot(pieces[...], jnp.concatenate([n0, n1], axis=1), preferred_element_type=F32)
        small = jnp.dot(pieces[:nx], n2, preferred_element_type=F32) + wide[nx : 2 * nx, rank:] + wide[2 * nx :, :rank]
        product = wide[:nx, :rank] + ((wide[:nx, rank:] + wide[nx : 2 * nx, :rank]) + small)
        cross = lax.dot_general(
            product, product, (((0,), (0,)), ((), ())), precision=HIGHEST, preferred_element_type=F32
        )
        inverse = inverse_factor(cross, work)
        now = lax.dot_general(
            product, inverse, (((1,), (1,)), ((), ())), precision=HIGHEST, preferred_element_type=F32
        )
    basis[...] = now
    turned[...] = now.T


def project_kernel(
    where, turned, own0, near0, far2, far3, own2, near2, ahead2, ahead3, mine, mine2, to1, to2, to3
):
    here = where[0]
    cells_y, rows, _ = own0.shape
    early = ahead2.shape[0]
    rank = turned.shape[0]
    share = rank // 4
    lines = []
    for k in range(4):
        line = pl.ds(pl.multiple_of((here ^ k) * share, share), share)
        cols = [turned[line, pl.ds(pl.multiple_of((here ^ i) * rows, rows), rows)] for i in range(4)]
        lines.append(jnp.concatenate(cols, axis=1))
    b_hi, b_lo = split(jnp.concatenate(lines, axis=0))

    def planes(count, sources):
        both = jnp.concatenate([b_hi[:count], b_lo[:count]], axis=0)
        f_hi, f_lo = split(jnp.concatenate(sources, axis=0))
        with_hi = jnp.dot(both, f_hi, preferred_element_type=F32)
        with_lo = jnp.dot(b_hi[:count], f_lo, preferred_element_type=F32)
        return with_hi[:count] + with_hi[count:] + with_lo

    for y in range(cells_y):
        total = planes(rank if y >= early else 2 * share, [own0[y], near0[y], far2[y], far3[y]])
        mine[y] = total[:share]
        to1[y] = total[share : 2 * share]
        if y >= early:
            to2[y - early] = total[2 * share : 3 * share]
            to3[y - early] = total[3 * share :]
    for y in range(early):
        total = planes(2 * share, [own2[y], near2[y], ahead2[y], ahead3[y]])
        mine2[y] = total[:share]
        to1[cells_y + y] = total[share:]


def call(kernel, outs, scratch, scalars, args, flops, moved):
    smem = pl.BlockSpec(memory_space=pltpu.SMEM)
    vmem = pl.BlockSpec(memory_space=pltpu.VMEM)
    return pl.pallas_call(
        kernel,
        out_shape=outs,
        in_specs=[smem] * len(scalars) + [vmem] * len(args),
        out_specs=jax.tree.map(lambda _: vmem, outs),
        scratch_shapes=scratch,
        compiler_params=pltpu.CompilerParams(vmem_limit_bytes=VMEM_LIMIT),
        cost_estimate=pl.CostEstimate(flops=flops, bytes_accessed=moved, transcendentals=0),
    )(*scalars, *args)


def as_it_lies(value):
    return with_layout_constraint(value, Layout(major_to_minor=tuple(range(value.ndim))))


def swap(value, axis, bit):
    return lax.ppermute(value, axis, [(i, i ^ bit) for i in range(lax.axis_size(axis))])


def local(field, start):
    spec_count, rows, cols_y, cells_z = field.shape
    n = lax.axis_index("narrow")
    core = n % 2
    chip = n // 2
    wide = lax.axis_size("wide")
    count = spec_count * cols_y * cells_z * wide
    where = n.reshape(1).astype(jnp.int32)
    shape = jax.ShapeDtypeStruct

    def species(array, k):
        return lax.dynamic_index_in_dim(array, n ^ k, 0, keepdims=False)

    def by_y(array):
        return jnp.swapaxes(array, 0, 1)

    f2 = by_y(species(field, 2))
    far2 = swap(f2, "narrow", 2)
    rest, f2 = lax.optimization_barrier((field, f2))
    f0, f1, f3 = (species(rest, k) for k in (0, 1, 3))
    near0 = by_y(as_it_lies(swap(as_it_lies(f1), "narrow", 1)))
    near2 = by_y(as_it_lies(swap(as_it_lies(f3), "narrow", 1)))
    f0 = by_y(f0)
    f3 = by_y(f3)

    half = 2 * rows
    strip = shape((rows, half), F32)
    acc2 = pltpu.VMEM((half, rows), F32)
    acc = pltpu.VMEM((half, half), F32)
    keep, send = call(
        same_kernel, (strip, strip), [acc, acc], [where], [f0, f2, near0, near2],
        2 * 2 * half * half * 2 * cols_y * cells_z, 8 * rows * cols_y * cells_z * 4,
    )
    steps = [("wide", 1), ("wide", 2), ("wide", 8), ("wide", 16)]

    def place(axis, bit):
        index = core if axis == "narrow" else lax.axis_index("wide") // bit
        return index % 2

    path = [("narrow", 1)] + steps
    part = keep + swap(send, "narrow", 1)
    for axis, bit in steps:
        size = part.shape[0] // 2
        mine = place(axis, bit)
        keep = lax.dynamic_slice_in_dim(part, mine * size, size)
        part = keep + swap(lax.dynamic_slice_in_dim(part, (1 - mine) * size, size), axis, bit)
    group = lax.axis_size("narrow")
    across = [(i, i ^ 2 ^ (4 * group)) for i in range(wide * group)]
    peer = swap(part, "narrow", 2)
    twin = swap(part, "wide", 4)
    peer_twin = lax.ppermute(part, ("wide", "narrow"), across)
    peer, twin, peer_twin, far2, f3 = lax.optimization_barrier((peer, twin, peer_twin, far2, f3))
    twin = part + twin
    peer = peer + peer_twin
    both = jnp.stack([twin, peer])
    far3 = swap(f3, "narrow", 3)
    for axis, bit in path[::-1]:
        other = swap(both, axis, bit)
        low = place(axis, bit) == 0
        both = jnp.concatenate([jnp.where(low, both, other), jnp.where(low, other, both)], axis=1)
    both, far3 = lax.optimization_barrier((both, far3))
    g00 = jnp.where(chip == 0, both[0], both[1])
    g11 = jnp.where(chip == 0, both[1], both[0])

    block2 = call(
        block_kernel, shape((half, rows), F32), [acc2, acc2], [], [f0, near0, far2],
        2 * 3 * half * rows * cols_y * cells_z, 6 * rows * cols_y * cells_z * 4,
    )
    block2, far3 = lax.optimization_barrier((block2, far3))
    keep, send = call(
        other_kernel, (strip, strip), [acc2, acc2], [where], [f0, near0, far3, block2],
        2 * 3 * half * rows * cols_y * cells_z, 6 * rows * cols_y * cells_z * 4,
    )
    part = keep + swap(send, "narrow", 1)
    part = part + swap(part, "narrow", 2)
    part = part + swap(part, "wide", 4)
    early = cols_y // 2
    part, first0, first1 = lax.optimization_barrier((part, f0[:early], by_y(f1)[:early]))
    ahead2 = swap(first0, "narrow", 2)
    ahead3 = swap(first1, "narrow", 3)
    for axis, bit in steps:
        part = part + swap(part, axis, bit)
    part, ahead2 = lax.optimization_barrier((part, ahead2))
    other = swap(part, "narrow", 1)
    g01 = jnp.concatenate([jnp.where(core == 0, part, other), jnp.where(core == 0, other, part)], axis=0)

    nx, rank = start.shape
    iterate = lambda *refs: iterate_kernel(count, *refs)
    basis, turned = call(
        iterate, (shape((nx, rank), F32), shape((rank, nx), F32)), [pltpu.VMEM((3 * nx, nx), BF16), pltpu.VMEM((rank, 2 * rank), F32)],
        [], [g00, g11, g01, start], 2 * 6 * 3 * nx * nx * rank, 4 * nx * nx,
    )

    share = rank // 4
    plane = lambda count: shape((count, share, cells_z), F32)
    mine, mine2, to1, to2, to3 = call(
        project_kernel,
        (plane(cols_y), plane(early), plane(cols_y + early), plane(cols_y - early), plane(cols_y - early)),
        [], [where], [turned, f0, near0, far2, far3, f2, near2, ahead2, ahead3],
        2 * 3 * rank * nx * cols_y * cells_z, nx * cols_y * cells_z * 4,
    )
    from2 = swap(to2, "narrow", 2)
    from3 = swap(to3, "narrow", 3)
    from1 = swap(to1, "narrow", 1)
    core_out = jnp.zeros((share, spec_count, cols_y, cells_z), F32)
    pieces = (
        mine,
        from1[:cols_y],
        jnp.concatenate([mine2, from2], axis=0),
        jnp.concatenate([from1[cols_y:], from3], axis=0),
    )
    for k, piece in enumerate(pieces):
        core_out = lax.dynamic_update_slice_in_dim(core_out, by_y(piece)[:, None], n ^ k, axis=1)
    return (basis, core_out)


def solution(mesh):
    return jax.shard_map(
        local,
        mesh=mesh,
        in_specs=(P(None, "narrow", "wide", None), P()),
        out_specs=(P(), P("narrow", None, "wide", None)),
        check_vma=False,
    )
```

```python
import jax
import jax.numpy as jnp
from jax import lax
from jax.experimental import pallas as pl
from jax.experimental.layout import Layout, with_layout_constraint
from jax.experimental.pallas import tpu as pltpu
from jax.sharding import PartitionSpec as P

ITERS = 3
HIGHEST = lax.Precision.HIGHEST
F32 = jnp.float32
BF16 = jnp.bfloat16
VMEM_LIMIT = 24 * 1024 * 1024


def contract_lanes(a, b):
    return lax.dot_general(a, b, (((1,), (1,)), ((), ())), preferred_element_type=F32)


def split(value):
    hi = value.astype(BF16)
    return hi, (value - hi.astype(F32)).astype(BF16)


def pair(first, second):
    return split(jnp.concatenate([first, second], axis=0))


def store_in_order(keep, send, total, swapped, turned):
    half = total.shape[0] // 2
    for core in (0, 1):
        for turn in (0, 1):

            @pl.when((swapped == core) & (turned == turn))
            def _(core=core, turn=turn):
                value = total.T if turn else total
                for out, rows in ((keep, value[:half]), (send, value[half:])):
                    if core:
                        out[:, :half] = rows[:, half:]
                        out[:, half:] = rows[:, :half]
                    else:
                        out[...] = rows


def same_kernel(where, own0, own2, near0, near2, keep, send, main, cross):
    main[...] = jnp.zeros_like(main)
    cross[...] = jnp.zeros_like(cross)
    for own, near in ((own0, near0), (own2, near2)):
        for y in range(own.shape[0]):
            hi, lo = pair(own[y], near[y])
            main[...] += contract_lanes(hi, hi)
            cross[...] += contract_lanes(hi, lo)
    store_in_order(keep, send, main[...] + cross[...] + cross[...].T, where[0] % 2, 0)


def block_planes(own, near, fars, out, main, cross):
    main[...] = jnp.zeros_like(main)
    cross[...] = jnp.zeros_like(cross)
    at = 0
    for far in fars:
        for y in range(far.shape[0]):
            hi, lo = pair(own[at], near[at])
            far_hi, far_lo = split(far[y])
            main[...] += contract_lanes(hi, far_hi)
            cross[...] += contract_lanes(hi, far_lo)
            cross[...] += contract_lanes(lo, far_hi)
            at += 1
    out[...] = main[...] + cross[...]


def block_kernel(own, near, far, out, main, cross):
    block_planes(own, near, (far,), out, main, cross)


def other_kernel(where, own, near, far3a, far3b, block2, keep, send, main, cross):
    block_planes(own, near, (far3a, far3b), main, main, cross)
    total = jnp.concatenate([block2[...], main[...]], axis=1)
    store_in_order(keep, send, total, where[0] % 2, where[0] // 2)


PANEL = 32


def panel(rows, inverse, base):
    count = len(rows)
    shape = rows[0].shape
    sub = lax.broadcasted_iota(jnp.int32, shape, 0)
    size = 8 * count
    cols = [[jnp.broadcast_to(block[:, base + m : base + m + 1], shape) for block in rows] for m in range(size)]
    pivots = [jnp.ones(shape, F32) for _ in range(count)]

    def line(block, row):
        return jnp.broadcast_to(block[row : row + 1], shape)

    for j in range(size):
        at, row = divmod(j, 8)
        pivot = line(cols[j][at], row)
        pivots[at] = jnp.where(sub == row, pivot, pivots[at])
        if j == size - 1:
            break
        reciprocal = 1.0 / pivot
        row_line, inverse_line = line(rows[at], row), line(inverse[at], row)
        col_lines = {m: line(cols[m][at], row) for m in range(j + 1, size)}
        for b in range((j + 1) // 8, count):
            factor = cols[j][b] * reciprocal
            if b == at:
                factor = jnp.where(sub > row, factor, 0.0)
            for m in range(j + 1, size):
                cols[m][b] = cols[m][b] - factor * col_lines[m]
            rows[b] = rows[b] - factor * row_line
            inverse[b] = inverse[b] - factor * inverse_line
    scales = [lax.rsqrt(p) for p in pivots]
    joined = lambda blocks: jnp.concatenate([b * s for b, s in zip(blocks, scales)], axis=0)
    return joined(rows), joined(inverse)


def inverse_factor(cross, work):
    rank = cross.shape[0]
    row = lax.broadcasted_iota(jnp.int32, cross.shape, 0)
    col = lax.broadcasted_iota(jnp.int32, cross.shape, 1)
    work[:, :rank] = cross
    work[:, rank:] = jnp.where(row == col, 1.0, 0.0)
    for base in range(0, rank, PANEL):
        starts = range(base, base + PANEL, 8)
        upper, inverse = panel([work[i : i + 8, :rank] for i in starts], [work[i : i + 8, rank:] for i in starts], base)
        after = base + PANEL
        work[base:after, rank:] = inverse
        if after < rank:
            both = jnp.concatenate([upper, inverse], axis=1)
            work[after:, :] -= lax.dot_general(
                upper[:, after:], both, (((0,), (0,)), ((), ())), precision=HIGHEST, preferred_element_type=F32
            )
    return work[:, rank:]


def split3(value):
    first = value.astype(BF16)
    rest = value - first.astype(F32)
    second = rest.astype(BF16)
    return first, second, (rest - second.astype(F32)).astype(BF16)


def iterate_kernel(count, g00, g11, g01, start, basis, turned, pieces, work):
    nx, rank = start.shape
    half = nx // 2
    scale = 1.0 / count
    blocks = ((0, 0, g00[...]), (1, 1, g11[...]), (0, 1, g01[...]), (1, 0, g01[...].T))
    for i, j, block in blocks:
        for k, piece in enumerate(split3(block * scale)):
            row = k * nx + i * half
            pieces[row : row + half, j * half : (j + 1) * half] = piece
    now = start[...]
    for _ in range(ITERS):
        n0, n1, n2 = split3(now)
        wide = jnp.dot(pieces[...], jnp.concatenate([n0, n1], axis=1), preferred_element_type=F32)
        small = jnp.dot(pieces[:nx], n2, preferred_element_type=F32) + wide[nx : 2 * nx, rank:] + wide[2 * nx :, :rank]
        product = wide[:nx, :rank] + ((wide[:nx, rank:] + wide[nx : 2 * nx, :rank]) + small)
        cross = lax.dot_general(
            product, product, (((0,), (0,)), ((), ())), precision=HIGHEST, preferred_element_type=F32
        )
        inverse = inverse_factor(cross, work)
        now = lax.dot_general(
            product, inverse, (((1,), (1,)), ((), ())), precision=HIGHEST, preferred_element_type=F32
        )
    basis[...] = now
    turned[...] = now.T


def project_kernel(
    where, turned, own0, near0, far2, far3a, far3b, own2, near2, ahead2, ahead3, mine, mine2, to1, to2, to3
):
    here = where[0]
    cells_y, rows, _ = own0.shape
    early = ahead2.shape[0]
    rank = turned.shape[0]
    share = rank // 4
    lines = []
    for k in range(4):
        line = pl.ds(pl.multiple_of((here ^ k) * share, share), share)
        cols = [turned[line, pl.ds(pl.multiple_of((here ^ i) * rows, rows), rows)] for i in range(4)]
        lines.append(jnp.concatenate(cols, axis=1))
    b_hi, b_lo = split(jnp.concatenate(lines, axis=0))

    def planes(count, sources):
        both = jnp.concatenate([b_hi[:count], b_lo[:count]], axis=0)
        f_hi, f_lo = split(jnp.concatenate(sources, axis=0))
        with_hi = jnp.dot(both, f_hi, preferred_element_type=F32)
        with_lo = jnp.dot(b_hi[:count], f_lo, preferred_element_type=F32)
        return with_hi[:count] + with_hi[count:] + with_lo

    for y in range(cells_y):
        cut = far3a.shape[0]
        far3 = far3a[y] if y < cut else far3b[y - cut]
        total = planes(rank if y >= early else 2 * share, [own0[y], near0[y], far2[y], far3])
        mine[y] = total[:share]
        to1[y] = total[share : 2 * share]
        if y >= early:
            to2[y - early] = total[2 * share : 3 * share]
            to3[y - early] = total[3 * share :]
    for y in range(early):
        total = planes(2 * share, [own2[y], near2[y], ahead2[y], ahead3[y]])
        mine2[y] = total[:share]
        to1[cells_y + y] = total[share:]


def call(kernel, outs, scratch, scalars, args, flops, moved):
    smem = pl.BlockSpec(memory_space=pltpu.SMEM)
    vmem = pl.BlockSpec(memory_space=pltpu.VMEM)
    return pl.pallas_call(
        kernel,
        out_shape=outs,
        in_specs=[smem] * len(scalars) + [vmem] * len(args),
        out_specs=jax.tree.map(lambda _: vmem, outs),
        scratch_shapes=scratch,
        compiler_params=pltpu.CompilerParams(vmem_limit_bytes=VMEM_LIMIT),
        cost_estimate=pl.CostEstimate(flops=flops, bytes_accessed=moved, transcendentals=0),
    )(*scalars, *args)


def as_it_lies(value):
    return with_layout_constraint(value, Layout(major_to_minor=tuple(range(value.ndim))))


def swap(value, axis, bit):
    return lax.ppermute(value, axis, [(i, i ^ bit) for i in range(lax.axis_size(axis))])


def local(field, start):
    spec_count, rows, cols_y, cells_z = field.shape
    n = lax.axis_index("narrow")
    core = n % 2
    chip = n // 2
    wide = lax.axis_size("wide")
    count = spec_count * cols_y * cells_z * wide
    where = n.reshape(1).astype(jnp.int32)
    shape = jax.ShapeDtypeStruct

    def species(array, k):
        return lax.dynamic_index_in_dim(array, n ^ k, 0, keepdims=False)

    def by_y(array):
        return jnp.swapaxes(array, 0, 1)

    f2 = by_y(species(field, 2))
    far2 = swap(f2, "narrow", 2)
    rest, f2 = lax.optimization_barrier((field, f2))
    f0, f1, f3 = (species(rest, k) for k in (0, 1, 3))
    near0 = by_y(as_it_lies(swap(as_it_lies(f1), "narrow", 1)))
    near2 = by_y(as_it_lies(swap(as_it_lies(f3), "narrow", 1)))
    f0 = by_y(f0)
    f3 = by_y(f3)

    half = 2 * rows
    strip = shape((rows, half), F32)
    acc2 = pltpu.VMEM((half, rows), F32)
    acc = pltpu.VMEM((half, half), F32)
    keep, send = call(
        same_kernel, (strip, strip), [acc, acc], [where], [f0, f2, near0, near2],
        2 * 2 * half * half * 2 * cols_y * cells_z, 8 * rows * cols_y * cells_z * 4,
    )
    steps = [("wide", 1), ("wide", 2), ("wide", 8), ("wide", 16)]

    def place(axis, bit):
        index = core if axis == "narrow" else lax.axis_index("wide") // bit
        return index % 2

    path = [("narrow", 1)] + steps
    part = keep + swap(send, "narrow", 1)
    for axis, bit in steps:
        size = part.shape[0] // 2
        mine = place(axis, bit)
        keep = lax.dynamic_slice_in_dim(part, mine * size, size)
        part = keep + swap(lax.dynamic_slice_in_dim(part, (1 - mine) * size, size), axis, bit)
    group = lax.axis_size("narrow")
    across = [(i, i ^ 2 ^ (4 * group)) for i in range(wide * group)]
    cut = cols_y // 4
    part, f3 = lax.optimization_barrier((part, f3))
    peer = swap(part, "narrow", 2)
    twin = swap(part, "wide", 4)
    peer_twin = lax.ppermute(part, ("wide", "narrow"), across)
    far3a = swap(f3[:cut], "narrow", 3)
    peer, twin, peer_twin, far2, f3 = lax.optimization_barrier((peer, twin, peer_twin, far2, f3))
    twin = part + twin
    peer = peer + peer_twin
    both = jnp.stack([twin, peer])
    far3b = swap(f3[cut:], "narrow", 3)
    for axis, bit in path[::-1]:
        if bit == 8:
            both, far3a = lax.optimization_barrier((both, far3a))
        other = swap(both, axis, bit)
        low = place(axis, bit) == 0
        both = jnp.concatenate([jnp.where(low, both, other), jnp.where(low, other, both)], axis=1)
    both, far3b = lax.optimization_barrier((both, far3b))
    g00 = jnp.where(chip == 0, both[0], both[1])
    g11 = jnp.where(chip == 0, both[1], both[0])

    block2 = call(
        block_kernel, shape((half, rows), F32), [acc2, acc2], [], [f0, near0, far2],
        2 * 3 * half * rows * cols_y * cells_z, 6 * rows * cols_y * cells_z * 4,
    )
    block2, far3b = lax.optimization_barrier((block2, far3b))
    keep, send = call(
        other_kernel, (strip, strip), [acc2, acc2], [where], [f0, near0, far3a, far3b, block2],
        2 * 3 * half * rows * cols_y * cells_z, 6 * rows * cols_y * cells_z * 4,
    )
    part = keep + swap(send, "narrow", 1)
    part = part + swap(part, "narrow", 2)
    part = part + swap(part, "wide", 4)
    early = cols_y // 2
    part, first0, first1 = lax.optimization_barrier((part, f0[:early], by_y(f1)[:early]))
    ahead2 = swap(first0, "narrow", 2)
    ahead3 = swap(first1, "narrow", 3)
    for axis, bit in steps:
        part = part + swap(part, axis, bit)
    part, ahead2 = lax.optimization_barrier((part, ahead2))
    other = swap(part, "narrow", 1)
    g01 = jnp.concatenate([jnp.where(core == 0, part, other), jnp.where(core == 0, other, part)], axis=0)

    nx, rank = start.shape
    iterate = lambda *refs: iterate_kernel(count, *refs)
    basis, turned = call(
        iterate, (shape((nx, rank), F32), shape((rank, nx), F32)), [pltpu.VMEM((3 * nx, nx), BF16), pltpu.VMEM((rank, 2 * rank), F32)],
        [], [g00, g11, g01, start], 2 * 6 * 3 * nx * nx * rank, 4 * nx * nx,
    )

    share = rank // 4
    plane = lambda count: shape((count, share, cells_z), F32)
    mine, mine2, to1, to2, to3 = call(
        project_kernel,
        (plane(cols_y), plane(early), plane(cols_y + early), plane(cols_y - early), plane(cols_y - early)),
        [], [where], [turned, f0, near0, far2, far3a, far3b, f2, near2, ahead2, ahead3],
        2 * 3 * rank * nx * cols_y * cells_z, nx * cols_y * cells_z * 4,
    )
    from2 = swap(to2, "narrow", 2)
    from3 = swap(to3, "narrow", 3)
    from1 = swap(to1, "narrow", 1)
    core_out = jnp.zeros((share, spec_count, cols_y, cells_z), F32)
    pieces = (
        mine,
        from1[:cols_y],
        jnp.concatenate([mine2, from2], axis=0),
        jnp.concatenate([from1[cols_y:], from3], axis=0),
    )
    for k, piece in enumerate(pieces):
        core_out = lax.dynamic_update_slice_in_dim(core_out, by_y(piece)[:, None], n ^ k, axis=1)
    return (basis, core_out)


def solution(mesh):
    return jax.shard_map(
        local,
        mesh=mesh,
        in_specs=(P(None, "narrow", "wide", None), P()),
        out_specs=(P(), P("narrow", None, "wide", None)),
        check_vma=False,
    )
```

```python
import jax
import jax.numpy as jnp
from jax import lax
from jax.experimental import pallas as pl
from jax.experimental.layout import Layout, with_layout_constraint
from jax.experimental.pallas import tpu as pltpu
from jax.sharding import PartitionSpec as P

ITERS = 3
HIGHEST = lax.Precision.HIGHEST
F32 = jnp.float32
BF16 = jnp.bfloat16
VMEM_LIMIT = 24 * 1024 * 1024


def contract_lanes(a, b):
    return lax.dot_general(a, b, (((1,), (1,)), ((), ())), preferred_element_type=F32)


def split(value):
    hi = value.astype(BF16)
    return hi, (value - hi.astype(F32)).astype(BF16)


def pair(first, second):
    return split(jnp.concatenate([first, second], axis=0))


def store_in_order(keep, send, total, swapped, turned):
    half = total.shape[0] // 2
    for core in (0, 1):
        for turn in (0, 1):

            @pl.when((swapped == core) & (turned == turn))
            def _(core=core, turn=turn):
                value = total.T if turn else total
                for out, rows in ((keep, value[:half]), (send, value[half:])):
                    if core:
                        out[:, :half] = rows[:, half:]
                        out[:, half:] = rows[:, :half]
                    else:
                        out[...] = rows


def same_kernel(where, own0, own2, near0, near2, keep, send, main, cross):
    main[...] = jnp.zeros_like(main)
    cross[...] = jnp.zeros_like(cross)
    for own, near in ((own0, near0), (own2, near2)):
        for y in range(own.shape[0]):
            hi, lo = pair(own[y], near[y])
            main[...] += contract_lanes(hi, hi)
            cross[...] += contract_lanes(hi, lo)
    store_in_order(keep, send, main[...] + cross[...] + cross[...].T, where[0] % 2, 0)


def block_planes(own, near, fars, out, main, cross):
    main[...] = jnp.zeros_like(main)
    cross[...] = jnp.zeros_like(cross)
    at = 0
    for far in fars:
        for y in range(far.shape[0]):
            hi, lo = pair(own[at], near[at])
            far_hi, far_lo = split(far[y])
            main[...] += contract_lanes(hi, far_hi)
            cross[...] += contract_lanes(hi, far_lo)
            cross[...] += contract_lanes(lo, far_hi)
            at += 1
    out[...] = main[...] + cross[...]


def block_kernel(own, near, far, out, main, cross):
    block_planes(own, near, (far,), out, main, cross)


def other_kernel(where, own, near, far3a, far3b, block2, keep, send, main, cross):
    block_planes(own, near, (far3a, far3b), main, main, cross)
    total = jnp.concatenate([block2[...], main[...]], axis=1)
    store_in_order(keep, send, total, where[0] % 2, where[0] // 2)


PANEL = 32


def panel(rows, inverse, base):
    count = len(rows)
    shape = rows[0].shape
    sub = lax.broadcasted_iota(jnp.int32, shape, 0)
    size = 8 * count
    cols = [[jnp.broadcast_to(block[:, base + m : base + m + 1], shape) for block in rows] for m in range(size)]
    pivots = [jnp.ones(shape, F32) for _ in range(count)]

    def line(block, row):
        return jnp.broadcast_to(block[row : row + 1], shape)

    for j in range(size):
        at, row = divmod(j, 8)
        pivot = line(cols[j][at], row)
        pivots[at] = jnp.where(sub == row, pivot, pivots[at])
        if j == size - 1:
            break
        reciprocal = 1.0 / pivot
        row_line, inverse_line = line(rows[at], row), line(inverse[at], row)
        col_lines = {m: line(cols[m][at], row) for m in range(j + 1, size)}
        for b in range((j + 1) // 8, count):
            factor = cols[j][b] * reciprocal
            if b == at:
                factor = jnp.where(sub > row, factor, 0.0)
            for m in range(j + 1, size):
                cols[m][b] = cols[m][b] - factor * col_lines[m]
            rows[b] = rows[b] - factor * row_line
            inverse[b] = inverse[b] - factor * inverse_line
    scales = [lax.rsqrt(p) for p in pivots]
    joined = lambda blocks: jnp.concatenate([b * s for b, s in zip(blocks, scales)], axis=0)
    return joined(rows), joined(inverse)


def inverse_factor(cross, work):
    rank = cross.shape[0]
    row = lax.broadcasted_iota(jnp.int32, cross.shape, 0)
    col = lax.broadcasted_iota(jnp.int32, cross.shape, 1)
    work[:, :rank] = cross
    work[:, rank:] = jnp.where(row == col, 1.0, 0.0)
    for base in range(0, rank, PANEL):
        starts = range(base, base + PANEL, 8)
        upper, inverse = panel([work[i : i + 8, :rank] for i in starts], [work[i : i + 8, rank:] for i in starts], base)
        after = base + PANEL
        work[base:after, rank:] = inverse
        if after < rank:
            both = jnp.concatenate([upper, inverse], axis=1)
            work[after:, :] -= lax.dot_general(
                upper[:, after:], both, (((0,), (0,)), ((), ())), precision=HIGHEST, preferred_element_type=F32
            )
    return work[:, rank:]


def split3(value):
    first = value.astype(BF16)
    rest = value - first.astype(F32)
    second = rest.astype(BF16)
    return first, second, (rest - second.astype(F32)).astype(BF16)


def iterate_kernel(count, g00, g11, g01, start, basis, turned, pieces, work):
    nx, rank = start.shape
    half = nx // 2
    scale = 1.0 / count
    blocks = ((0, 0, g00[...]), (1, 1, g11[...]), (0, 1, g01[...]), (1, 0, g01[...].T))
    for i, j, block in blocks:
        for k, piece in enumerate(split3(block * scale)):
            row = k * nx + i * half
            pieces[row : row + half, j * half : (j + 1) * half] = piece
    now = start[...]
    for _ in range(ITERS):
        n0, n1, n2 = split3(now)
        wide = jnp.dot(pieces[...], jnp.concatenate([n0, n1], axis=1), preferred_element_type=F32)
        small = jnp.dot(pieces[:nx], n2, preferred_element_type=F32) + wide[nx : 2 * nx, rank:] + wide[2 * nx :, :rank]
        product = wide[:nx, :rank] + ((wide[:nx, rank:] + wide[nx : 2 * nx, :rank]) + small)
        cross = lax.dot_general(
            product, product, (((0,), (0,)), ((), ())), precision=HIGHEST, preferred_element_type=F32
        )
        inverse = inverse_factor(cross, work)
        now = lax.dot_general(
            product, inverse, (((1,), (1,)), ((), ())), precision=HIGHEST, preferred_element_type=F32
        )
    basis[...] = now
    turned[...] = now.T


def project_kernel(
    where, turned, own0, near0, far2, far3a, far3b, own2, near2, ahead2, ahead3, mine, mine2, to1, to2, to3
):
    here = where[0]
    cells_y, rows, _ = own0.shape
    early = ahead2.shape[0]
    rank = turned.shape[0]
    share = rank // 4
    lines = []
    for k in range(4):
        line = pl.ds(pl.multiple_of((here ^ k) * share, share), share)
        cols = [turned[line, pl.ds(pl.multiple_of((here ^ i) * rows, rows), rows)] for i in range(4)]
        lines.append(jnp.concatenate(cols, axis=1))
    b_hi, b_lo = split(jnp.concatenate(lines, axis=0))

    def planes(count, sources):
        both = jnp.concatenate([b_hi[:count], b_lo[:count]], axis=0)
        f_hi, f_lo = split(jnp.concatenate(sources, axis=0))
        with_hi = jnp.dot(both, f_hi, preferred_element_type=F32)
        with_lo = jnp.dot(b_hi[:count], f_lo, preferred_element_type=F32)
        return with_hi[:count] + with_hi[count:] + with_lo

    for y in range(cells_y):
        cut = far3a.shape[0]
        far3 = far3a[y] if y < cut else far3b[y - cut]
        total = planes(rank if y >= early else 2 * share, [own0[y], near0[y], far2[y], far3])
        mine[y] = total[:share]
        to1[y] = total[share : 2 * share]
        if y >= early:
            to2[y - early] = total[2 * share : 3 * share]
            to3[y - early] = total[3 * share :]
    for y in range(early):
        total = planes(2 * share, [own2[y], near2[y], ahead2[y], ahead3[y]])
        mine2[y] = total[:share]
        to1[cells_y + y] = total[share:]


def call(kernel, outs, scratch, scalars, args, flops, moved):
    smem = pl.BlockSpec(memory_space=pltpu.SMEM)
    vmem = pl.BlockSpec(memory_space=pltpu.VMEM)
    return pl.pallas_call(
        kernel,
        out_shape=outs,
        in_specs=[smem] * len(scalars) + [vmem] * len(args),
        out_specs=jax.tree.map(lambda _: vmem, outs),
        scratch_shapes=scratch,
        compiler_params=pltpu.CompilerParams(vmem_limit_bytes=VMEM_LIMIT),
        cost_estimate=pl.CostEstimate(flops=flops, bytes_accessed=moved, transcendentals=0),
    )(*scalars, *args)


def as_it_lies(value):
    return with_layout_constraint(value, Layout(major_to_minor=tuple(range(value.ndim))))


def swap(value, axis, bit):
    return lax.ppermute(value, axis, [(i, i ^ bit) for i in range(lax.axis_size(axis))])


def local(field, start):
    spec_count, rows, cols_y, cells_z = field.shape
    n = lax.axis_index("narrow")
    core = n % 2
    chip = n // 2
    wide = lax.axis_size("wide")
    count = spec_count * cols_y * cells_z * wide
    where = n.reshape(1).astype(jnp.int32)
    shape = jax.ShapeDtypeStruct

    def species(array, k):
        return lax.dynamic_index_in_dim(array, n ^ k, 0, keepdims=False)

    def by_y(array):
        return jnp.swapaxes(array, 0, 1)

    f2 = by_y(species(field, 2))
    far2 = swap(f2, "narrow", 2)
    rest, f2 = lax.optimization_barrier((field, f2))
    f0, f1, f3 = (species(rest, k) for k in (0, 1, 3))
    near0 = by_y(as_it_lies(swap(as_it_lies(f1), "narrow", 1)))
    near2 = by_y(as_it_lies(swap(as_it_lies(f3), "narrow", 1)))
    f0 = by_y(f0)
    f3 = by_y(f3)

    half = 2 * rows
    strip = shape((rows, half), F32)
    acc2 = pltpu.VMEM((half, rows), F32)
    acc = pltpu.VMEM((half, half), F32)
    keep, send = call(
        same_kernel, (strip, strip), [acc, acc], [where], [f0, f2, near0, near2],
        2 * 2 * half * half * 2 * cols_y * cells_z, 8 * rows * cols_y * cells_z * 4,
    )
    steps = [("wide", 1), ("wide", 2), ("wide", 8), ("wide", 16)]

    def place(axis, bit):
        index = core if axis == "narrow" else lax.axis_index("wide") // bit
        return index % 2

    path = [("narrow", 1)] + steps
    part = keep + swap(send, "narrow", 1)
    for axis, bit in steps:
        size = part.shape[0] // 2
        mine = place(axis, bit)
        keep = lax.dynamic_slice_in_dim(part, mine * size, size)
        part = keep + swap(lax.dynamic_slice_in_dim(part, (1 - mine) * size, size), axis, bit)
    group = lax.axis_size("narrow")
    across = [(i, i ^ 2 ^ (4 * group)) for i in range(wide * group)]
    cut = cols_y // 4
    part, f3 = lax.optimization_barrier((part, f3))
    peer = swap(part, "narrow", 2)
    twin = swap(part, "wide", 4)
    peer_twin = lax.ppermute(part, ("wide", "narrow"), across)
    far3a = swap(f3[:cut], "narrow", 3)
    peer, twin, peer_twin, far2, f3 = lax.optimization_barrier((peer, twin, peer_twin, far2, f3))
    twin = part + twin
    peer = peer + peer_twin
    both = jnp.stack([twin, peer])
    far3b = swap(f3[cut:], "narrow", 3)
    for axis, bit in path[::-1]:
        if bit == 8:
            both, far3a = lax.optimization_barrier((both, far3a))
        if axis == "narrow":
            both, far3b = lax.optimization_barrier((both, far3b))
        other = swap(both, axis, bit)
        low = place(axis, bit) == 0
        both = jnp.concatenate([jnp.where(low, both, other), jnp.where(low, other, both)], axis=1)
    g00 = jnp.where(chip == 0, both[0], both[1])
    g11 = jnp.where(chip == 0, both[1], both[0])

    block2 = call(
        block_kernel, shape((half, rows), F32), [acc2, acc2], [], [f0, near0, far2],
        2 * 3 * half * rows * cols_y * cells_z, 6 * rows * cols_y * cells_z * 4,
    )
    block2, far3b = lax.optimization_barrier((block2, far3b))
    keep, send = call(
        other_kernel, (strip, strip), [acc2, acc2], [where], [f0, near0, far3a, far3b, block2],
        2 * 3 * half * rows * cols_y * cells_z, 6 * rows * cols_y * cells_z * 4,
    )
    part = keep + swap(send, "narrow", 1)
    part = part + swap(part, "narrow", 2)
    part = part + swap(part, "wide", 4)
    early = cols_y // 2
    part, first0, first1 = lax.optimization_barrier((part, f0[:early], by_y(f1)[:early]))
    ahead2 = swap(first0, "narrow", 2)
    ahead3 = swap(first1, "narrow", 3)
    for axis, bit in steps:
        part = part + swap(part, axis, bit)
    part, ahead2 = lax.optimization_barrier((part, ahead2))
    other = swap(part, "narrow", 1)
    g01 = jnp.concatenate([jnp.where(core == 0, part, other), jnp.where(core == 0, other, part)], axis=0)

    nx, rank = start.shape
    iterate = lambda *refs: iterate_kernel(count, *refs)
    basis, turned = call(
        iterate, (shape((nx, rank), F32), shape((rank, nx), F32)), [pltpu.VMEM((3 * nx, nx), BF16), pltpu.VMEM((rank, 2 * rank), F32)],
        [], [g00, g11, g01, start], 2 * 6 * 3 * nx * nx * rank, 4 * nx * nx,
    )

    share = rank // 4
    plane = lambda count: shape((count, share, cells_z), F32)
    mine, mine2, to1, to2, to3 = call(
        project_kernel,
        (plane(cols_y), plane(early), plane(cols_y + early), plane(cols_y - early), plane(cols_y - early)),
        [], [where], [turned, f0, near0, far2, far3a, far3b, f2, near2, ahead2, ahead3],
        2 * 3 * rank * nx * cols_y * cells_z, nx * cols_y * cells_z * 4,
    )
    from2 = swap(to2, "narrow", 2)
    from3 = swap(to3, "narrow", 3)
    from1 = swap(to1, "narrow", 1)
    core_out = jnp.zeros((share, spec_count, cols_y, cells_z), F32)
    pieces = (
        mine,
        from1[:cols_y],
        jnp.concatenate([mine2, from2], axis=0),
        jnp.concatenate([from1[cols_y:], from3], axis=0),
    )
    for k, piece in enumerate(pieces):
        core_out = lax.dynamic_update_slice_in_dim(core_out, by_y(piece)[:, None], n ^ k, axis=1)
    return (basis, core_out)


def solution(mesh):
    return jax.shard_map(
        local,
        mesh=mesh,
        in_specs=(P(None, "narrow", "wide", None), P()),
        out_specs=(P(), P("narrow", None, "wide", None)),
        check_vma=False,
    )
```

```python
import jax
import jax.numpy as jnp
from jax import lax
from jax.experimental import pallas as pl
from jax.experimental.layout import Layout, with_layout_constraint
from jax.experimental.pallas import tpu as pltpu
from jax.sharding import PartitionSpec as P

ITERS = 3
HIGHEST = lax.Precision.HIGHEST
F32 = jnp.float32
BF16 = jnp.bfloat16
VMEM_LIMIT = 24 * 1024 * 1024


def contract_lanes(a, b):
    return lax.dot_general(a, b, (((1,), (1,)), ((), ())), preferred_element_type=F32)


def split(value):
    hi = value.astype(BF16)
    return hi, (value - hi.astype(F32)).astype(BF16)


def pair(first, second):
    return split(jnp.concatenate([first, second], axis=0))


def store_in_order(keep, send, total, swapped, turned):
    half = total.shape[0] // 2
    for core in (0, 1):
        for turn in (0, 1):

            @pl.when((swapped == core) & (turned == turn))
            def _(core=core, turn=turn):
                value = total.T if turn else total
                for out, rows in ((keep, value[:half]), (send, value[half:])):
                    if core:
                        out[:, :half] = rows[:, half:]
                        out[:, half:] = rows[:, :half]
                    else:
                        out[...] = rows


def same_kernel(where, own0, own2, near0, near2, keep, send, main, cross):
    main[...] = jnp.zeros_like(main)
    cross[...] = jnp.zeros_like(cross)
    for own, near in ((own0, near0), (own2, near2)):
        for y in range(own.shape[0]):
            hi, lo = pair(own[y], near[y])
            main[...] += contract_lanes(hi, hi)
            cross[...] += contract_lanes(hi, lo)
    store_in_order(keep, send, main[...] + cross[...] + cross[...].T, where[0] % 2, 0)


def block_planes(own, near, fars, out, main, cross):
    main[...] = jnp.zeros_like(main)
    cross[...] = jnp.zeros_like(cross)
    at = 0
    for far in fars:
        for y in range(far.shape[0]):
            hi, lo = pair(own[at], near[at])
            far_hi, far_lo = split(far[y])
            main[...] += contract_lanes(hi, far_hi)
            cross[...] += contract_lanes(hi, far_lo)
            cross[...] += contract_lanes(lo, far_hi)
            at += 1
    out[...] = main[...] + cross[...]


def block_kernel(own, near, far, out, main, cross):
    block_planes(own, near, (far,), out, main, cross)


def other_kernel(where, own, near, far3a, far3b, block2, keep, send, main, cross):
    block_planes(own, near, (far3a, far3b), main, main, cross)
    total = jnp.concatenate([block2[...], main[...]], axis=1)
    store_in_order(keep, send, total, where[0] % 2, where[0] // 2)


PANEL = 32


def panel(rows, inverse, base):
    count = len(rows)
    shape = rows[0].shape
    sub = lax.broadcasted_iota(jnp.int32, shape, 0)
    size = 8 * count
    cols = [[jnp.broadcast_to(block[:, base + m : base + m + 1], shape) for block in rows] for m in range(size)]
    pivots = [jnp.ones(shape, F32) for _ in range(count)]

    def line(block, row):
        return jnp.broadcast_to(block[row : row + 1], shape)

    for j in range(size):
        at, row = divmod(j, 8)
        pivot = line(cols[j][at], row)
        pivots[at] = jnp.where(sub == row, pivot, pivots[at])
        if j == size - 1:
            break
        reciprocal = 1.0 / pivot
        row_line, inverse_line = line(rows[at], row), line(inverse[at], row)
        col_lines = {m: line(cols[m][at], row) for m in range(j + 1, size)}
        for b in range((j + 1) // 8, count):
            factor = cols[j][b] * reciprocal
            if b == at:
                factor = jnp.where(sub > row, factor, 0.0)
            for m in range(j + 1, size):
                cols[m][b] = cols[m][b] - factor * col_lines[m]
            rows[b] = rows[b] - factor * row_line
            inverse[b] = inverse[b] - factor * inverse_line
    scales = [lax.rsqrt(p) for p in pivots]
    joined = lambda blocks: jnp.concatenate([b * s for b, s in zip(blocks, scales)], axis=0)
    return joined(rows), joined(inverse)


def inverse_factor(cross, work):
    rank = cross.shape[0]
    row = lax.broadcasted_iota(jnp.int32, cross.shape, 0)
    col = lax.broadcasted_iota(jnp.int32, cross.shape, 1)
    work[:, :rank] = cross
    work[:, rank:] = jnp.where(row == col, 1.0, 0.0)
    for base in range(0, rank, PANEL):
        starts = range(base, base + PANEL, 8)
        upper, inverse = panel([work[i : i + 8, :rank] for i in starts], [work[i : i + 8, rank:] for i in starts], base)
        after = base + PANEL
        work[base:after, rank:] = inverse
        if after < rank:
            both = jnp.concatenate([upper, inverse], axis=1)
            work[after:, :] -= lax.dot_general(
                upper[:, after:], both, (((0,), (0,)), ((), ())), precision=HIGHEST, preferred_element_type=F32
            )
    return work[:, rank:]


def split3(value):
    first = value.astype(BF16)
    rest = value - first.astype(F32)
    second = rest.astype(BF16)
    return first, second, (rest - second.astype(F32)).astype(BF16)


def iterate_kernel(count, g00, g11, g01, start, basis, turned, pieces, work):
    nx, rank = start.shape
    half = nx // 2
    scale = 1.0 / count
    blocks = ((0, 0, g00[...]), (1, 1, g11[...]), (0, 1, g01[...]), (1, 0, g01[...].T))
    for i, j, block in blocks:
        for k, piece in enumerate(split3(block * scale)):
            row = k * nx + i * half
            pieces[row : row + half, j * half : (j + 1) * half] = piece
    now = start[...]
    for _ in range(ITERS):
        n0, n1, n2 = split3(now)
        wide = jnp.dot(pieces[...], jnp.concatenate([n0, n1], axis=1), preferred_element_type=F32)
        small = jnp.dot(pieces[:nx], n2, preferred_element_type=F32) + wide[nx : 2 * nx, rank:] + wide[2 * nx :, :rank]
        product = wide[:nx, :rank] + ((wide[:nx, rank:] + wide[nx : 2 * nx, :rank]) + small)
        cross = lax.dot_general(
            product, product, (((0,), (0,)), ((), ())), precision=HIGHEST, preferred_element_type=F32
        )
        inverse = inverse_factor(cross, work)
        now = lax.dot_general(
            product, inverse, (((1,), (1,)), ((), ())), precision=HIGHEST, preferred_element_type=F32
        )
    basis[...] = now
    turned[...] = now.T


def project_kernel(
    where, turned, own0, near0, far2, far3a, far3b, own2, near2, ahead2, ahead3, mine, mine2, to1, to2, to3
):
    here = where[0]
    cells_y, rows, _ = own0.shape
    early = ahead2.shape[0]
    rank = turned.shape[0]
    share = rank // 4
    lines = []
    for k in range(4):
        line = pl.ds(pl.multiple_of((here ^ k) * share, share), share)
        cols = [turned[line, pl.ds(pl.multiple_of((here ^ i) * rows, rows), rows)] for i in range(4)]
        lines.append(jnp.concatenate(cols, axis=1))
    b_hi, b_lo = split(jnp.concatenate(lines, axis=0))

    def planes(count, sources):
        both = jnp.concatenate([b_hi[:count], b_lo[:count]], axis=0)
        f_hi, f_lo = split(jnp.concatenate(sources, axis=0))
        with_hi = jnp.dot(both, f_hi, preferred_element_type=F32)
        with_lo = jnp.dot(b_hi[:count], f_lo, preferred_element_type=F32)
        return with_hi[:count] + with_hi[count:] + with_lo

    for y in range(cells_y):
        cut = far3a.shape[0]
        far3 = far3a[y] if y < cut else far3b[y - cut]
        total = planes(rank if y >= early else 2 * share, [own0[y], near0[y], far2[y], far3])
        mine[y] = total[:share]
        to1[y] = total[share : 2 * share]
        if y >= early:
            to2[y - early] = total[2 * share : 3 * share]
            to3[y - early] = total[3 * share :]
    for y in range(early):
        total = planes(2 * share, [own2[y], near2[y], ahead2[y], ahead3[y]])
        mine2[y] = total[:share]
        to1[cells_y + y] = total[share:]


def call(kernel, outs, scratch, scalars, args, flops, moved):
    smem = pl.BlockSpec(memory_space=pltpu.SMEM)
    vmem = pl.BlockSpec(memory_space=pltpu.VMEM)
    return pl.pallas_call(
        kernel,
        out_shape=outs,
        in_specs=[smem] * len(scalars) + [vmem] * len(args),
        out_specs=jax.tree.map(lambda _: vmem, outs),
        scratch_shapes=scratch,
        compiler_params=pltpu.CompilerParams(vmem_limit_bytes=VMEM_LIMIT),
        cost_estimate=pl.CostEstimate(flops=flops, bytes_accessed=moved, transcendentals=0),
    )(*scalars, *args)


def as_it_lies(value):
    return with_layout_constraint(value, Layout(major_to_minor=tuple(range(value.ndim))))


def swap(value, axis, bit):
    return lax.ppermute(value, axis, [(i, i ^ bit) for i in range(lax.axis_size(axis))])


def local(field, start):
    spec_count, rows, cols_y, cells_z = field.shape
    n = lax.axis_index("narrow")
    core = n % 2
    chip = n // 2
    wide = lax.axis_size("wide")
    count = spec_count * cols_y * cells_z * wide
    where = n.reshape(1).astype(jnp.int32)
    shape = jax.ShapeDtypeStruct

    def species(array, k):
        return lax.dynamic_index_in_dim(array, n ^ k, 0, keepdims=False)

    def by_y(array):
        return jnp.swapaxes(array, 0, 1)

    f2 = by_y(species(field, 2))
    far2 = swap(f2, "narrow", 2)
    rest, f2 = lax.optimization_barrier((field, f2))
    f0, f1, f3 = (species(rest, k) for k in (0, 1, 3))
    near0 = by_y(as_it_lies(swap(as_it_lies(f1), "narrow", 1)))
    near2 = by_y(as_it_lies(swap(as_it_lies(f3), "narrow", 1)))
    f0 = by_y(f0)
    f3 = by_y(f3)

    half = 2 * rows
    strip = shape((rows, half), F32)
    acc2 = pltpu.VMEM((half, rows), F32)
    acc = pltpu.VMEM((half, half), F32)
    keep, send = call(
        same_kernel, (strip, strip), [acc, acc], [where], [f0, f2, near0, near2],
        2 * 2 * half * half * 2 * cols_y * cells_z, 8 * rows * cols_y * cells_z * 4,
    )
    steps = [("wide", 1), ("wide", 2), ("wide", 8), ("wide", 16)]

    def place(axis, bit):
        index = core if axis == "narrow" else lax.axis_index("wide") // bit
        return index % 2

    path = [("narrow", 1)] + steps
    part = keep + swap(send, "narrow", 1)
    for axis, bit in steps:
        size = part.shape[0] // 2
        mine = place(axis, bit)
        keep = lax.dynamic_slice_in_dim(part, mine * size, size)
        part = keep + swap(lax.dynamic_slice_in_dim(part, (1 - mine) * size, size), axis, bit)
    group = lax.axis_size("narrow")
    across = [(i, i ^ 2 ^ (4 * group)) for i in range(wide * group)]
    cut = cols_y // 4
    part, f3 = lax.optimization_barrier((part, f3))
    peer = swap(part, "narrow", 2)
    twin = swap(part, "wide", 4)
    peer_twin = lax.ppermute(part, ("wide", "narrow"), across)
    far3a = swap(f3[:cut], "narrow", 3)
    peer, twin, peer_twin, far2, f3 = lax.optimization_barrier((peer, twin, peer_twin, far2, f3))
    twin = part + twin
    peer = peer + peer_twin
    both = jnp.stack([twin, peer])
    far3b = swap(f3[cut:], "narrow", 3)
    for axis, bit in path[::-1]:
        if bit == 8:
            both, far3a = lax.optimization_barrier((both, far3a))
        if axis == "narrow":
            both, far3b = lax.optimization_barrier((both, far3b))
        other = swap(both, axis, bit)
        low = place(axis, bit) == 0
        both = jnp.concatenate([jnp.where(low, both, other), jnp.where(low, other, both)], axis=1)
    g00 = jnp.where(chip == 0, both[0], both[1])
    g11 = jnp.where(chip == 0, both[1], both[0])

    block2 = call(
        block_kernel, shape((half, rows), F32), [acc2, acc2], [], [f0, near0, far2],
        2 * 3 * half * rows * cols_y * cells_z, 6 * rows * cols_y * cells_z * 4,
    )
    early = cols_y // 2
    first0, first1 = f0[:early], by_y(f1)[:early]
    block2, far3b, first0, first1 = lax.optimization_barrier((block2, far3b, first0, first1))
    keep, send = call(
        other_kernel, (strip, strip), [acc2, acc2], [where], [f0, near0, far3a, far3b, block2],
        2 * 3 * half * rows * cols_y * cells_z, 6 * rows * cols_y * cells_z * 4,
    )
    part = keep + swap(send, "narrow", 1)
    part = part + swap(part, "narrow", 2)
    part = part + swap(part, "wide", 4)
    part, first0, first1 = lax.optimization_barrier((part, first0, first1))
    ahead2 = swap(first0, "narrow", 2)
    ahead3 = swap(first1, "narrow", 3)
    for axis, bit in steps:
        part = part + swap(part, axis, bit)
    part, ahead2 = lax.optimization_barrier((part, ahead2))
    other = swap(part, "narrow", 1)
    g01 = jnp.concatenate([jnp.where(core == 0, part, other), jnp.where(core == 0, other, part)], axis=0)

    nx, rank = start.shape
    iterate = lambda *refs: iterate_kernel(count, *refs)
    basis, turned = call(
        iterate, (shape((nx, rank), F32), shape((rank, nx), F32)), [pltpu.VMEM((3 * nx, nx), BF16), pltpu.VMEM((rank, 2 * rank), F32)],
        [], [g00, g11, g01, start], 2 * 6 * 3 * nx * nx * rank, 4 * nx * nx,
    )

    share = rank // 4
    plane = lambda count: shape((count, share, cells_z), F32)
    mine, mine2, to1, to2, to3 = call(
        project_kernel,
        (plane(cols_y), plane(early), plane(cols_y + early), plane(cols_y - early), plane(cols_y - early)),
        [], [where], [turned, f0, near0, far2, far3a, far3b, f2, near2, ahead2, ahead3],
        2 * 3 * rank * nx * cols_y * cells_z, nx * cols_y * cells_z * 4,
    )
    from2 = swap(to2, "narrow", 2)
    from3 = swap(to3, "narrow", 3)
    from1 = swap(to1, "narrow", 1)
    core_out = jnp.zeros((share, spec_count, cols_y, cells_z), F32)
    pieces = (
        mine,
        from1[:cols_y],
        jnp.concatenate([mine2, from2], axis=0),
        jnp.concatenate([from1[cols_y:], from3], axis=0),
    )
    for k, piece in enumerate(pieces):
        core_out = lax.dynamic_update_slice_in_dim(core_out, by_y(piece)[:, None], n ^ k, axis=1)
    return (basis, core_out)


def solution(mesh):
    return jax.shard_map(
        local,
        mesh=mesh,
        in_specs=(P(None, "narrow", "wide", None), P()),
        out_specs=(P(), P("narrow", None, "wide", None)),
        check_vma=False,
    )
```
